32 devices in a mesh: tm: 4 (over x, core), row: 4 (over z), col: 2 (over y).
Axes of the slice: x: 2, y: 2, z: 4, core: 2. Of those that a mesh axis runs over, the one named last changes fastest.
Arguments:
- records: bfloat16 [192, 2, 16, 2048], P('tm', None, None, ('row', 'col')), may hold values from -6 to 6
- offsets: int32 [8, 8], replicated, may hold values from 0 to 3
Outputs:
- cthree: bfloat16 [2, 16, 2048, 2048], P(None, 'tm', 'row', 'col')
The draws below stay inside these ranges and needn't reach their ends.
All inputs are finite; a program needn't handle non-finite values.
Results may differ from the reference program's by a relative error of at most 0.017.
Values may be sent and summed in bfloat16 or wider, within the bound.
A program may use at most 192 MiB of HBM per device.

```python
import math
import jax
import jax.numpy as jnp
from jax import lax

S = 2048
F = 16
REC_DEV = 48
BLOCK = 256
NOFF = 4
RECORDS = 192
NB = 8
N_TM = 4


def place_ends(drawn, own_key, smallest, largest):
    longest = drawn.shape.index(max(drawn.shape))
    spots = []
    for shift in (0, 1):
        where = [jax.random.randint(jax.random.fold_in(own_key, axis), (), 0, length) for axis, length in enumerate(drawn.shape)]
        where[longest] = (where[longest] + shift) % drawn.shape[longest]
        spots.append(tuple(where))
    return drawn.at[spots[0]].set(smallest).at[spots[1]].set(largest)


def block_levels(stream_key, shape, split, smallest, largest):
    factor_of = 1.0
    for dim, blocks in split:
        steps = jax.random.uniform(jax.random.fold_in(jax.random.fold_in(stream_key, 6), dim), (blocks,), jnp.float32, smallest / len(split), largest / len(split))
        factor_of = factor_of * jnp.repeat(jnp.exp(steps), shape[dim] // blocks).reshape((-1,) + (1,) * (len(shape) - 1 - dim))
    return factor_of


def noise(rng, shape, width, limit, pieces=(), kind=jnp.bfloat16):
    factor_of = block_levels(rng, shape, pieces, -0.22, 0.18) if pieces else 1.0
    values = jax.random.normal(rng, shape, jnp.float32) * width * factor_of
    return jnp.minimum(jnp.maximum(values, -limit), limit).astype(kind)


def setup_inputs(seed: int = 0) -> dict:
    keys = jax.random.split(jax.random.key(seed), 3)
    records = noise(keys[0], (RECORDS, 2, F, S), 1.0, 6.0, ((0, 4), (3, 8)))
    offsets = place_ends(jax.random.randint(keys[1], (NB, NB), 0, NOFF), jax.random.fold_in(keys[1], 1), 0, NOFF - 1).astype(jnp.int32)
    return dict(records=records, offsets=offsets)


def lag_kernels(bins, count):
    freq = jnp.arange(bins, dtype=jnp.int32)
    lag = jnp.minimum(freq, bins - freq)
    starts = jnp.arange(count, dtype=jnp.int32)[:, None] + 2
    inside = (lag[None, :] >= starts) & (lag[None, :] < starts + 3)
    weights = jnp.where(inside, jnp.float32(1.0), jnp.float32(0.1))
    phase = (freq[:, None, None] - freq[None, :, None]) * freq[None, None, :] % bins
    cosines = jnp.cos(phase.astype(jnp.float32) * jnp.float32(2.0 * math.pi / bins))
    return jnp.einsum('ot,fgt->ofg', weights, cosines, precision=lax.Precision.HIGHEST) / jnp.float32(bins)

def gram_bin(xbin):
    grouped = xbin.reshape(N_TM, REC_DEV, 2, S)
    total = jnp.zeros((2, S, S), jnp.float32)
    for group in range(N_TM):
        piece = grouped[group]
        left = jnp.concatenate([piece[:, 0], piece[:, 1]], axis=0)
        right_imag = jnp.concatenate([piece[:, 1], -piece[:, 0]], axis=0)
        real_part = jnp.dot(left.T, left, preferred_element_type=jnp.float32)
        imag_part = jnp.dot(left.T, right_imag, preferred_element_type=jnp.float32)
        term = jnp.stack([real_part, imag_part]) / jnp.float32(math.sqrt(RECORDS))
        rounded = lax.optimization_barrier(term.astype(jnp.bfloat16))
        total = total + rounded.astype(jnp.float32)
    return total

def reference(records, offsets):
    gram = lax.map(gram_bin, jnp.moveaxis(records, 2, 0))
    gram = jnp.moveaxis(gram, 0, 1)
    lagged = lag_kernels(F, NOFF)
    symmetric = (offsets + offsets.T) % NOFF
    blocks = jnp.moveaxis(gram.reshape(2, F, NB, BLOCK, S), 2, 0)

    def window_block(args):
        block, block_index = args
        shift_cols = jnp.repeat(symmetric[block_index], BLOCK)
        result = jnp.zeros_like(block)
        for offset in range(NOFF):
            term = jnp.einsum('fg,cgab->cfab', lagged[offset], block, precision=lax.Precision.HIGHEST)
            result = result + jnp.where(shift_cols[None, None, None, :] == offset, term, jnp.float32(0.0))
        return result.astype(jnp.bfloat16)
    windowed = lax.map(window_block, (blocks, jnp.arange(NB, dtype=jnp.int32)))
    windowed = jnp.moveaxis(windowed, 0, 2).reshape(2, F, S, S)

    def square_bin(matrix):
        left = jnp.concatenate([matrix[0], matrix[1]], axis=1)
        right_real = jnp.concatenate([matrix[0], -matrix[1]], axis=0)
        right_imag = jnp.concatenate([matrix[1], matrix[0]], axis=0)
        real_part = jnp.dot(left, right_real, preferred_element_type=jnp.float32)
        imag_part = jnp.dot(left, right_imag, preferred_element_type=jnp.float32)
        return (jnp.stack([real_part, imag_part]) / jnp.float32(math.sqrt(S))).astype(jnp.bfloat16)
    cthree = lax.map(square_bin, jnp.moveaxis(windowed, 1, 0))
    return jnp.moveaxis(cthree, 0, 1)
```

```python
import functools
import math

import jax
import jax.numpy as jnp
import numpy as np
from jax import lax
from jax.experimental import pallas as pl
from jax.experimental.pallas import tpu as pltpu
from jax.sharding import PartitionSpec as P

BLOCK = 256
NOFF = 4
SUB = 16


def lag_table(bins):
    freq = np.arange(bins)
    lag = np.minimum(freq, bins - freq)
    starts = np.arange(NOFF)[:, None] + 2
    inside = (lag[None, :] >= starts) & (lag[None, :] < starts + 3)
    weights = np.where(inside, 1.0, 0.1)
    phase = (freq[:, None, None] - freq[None, :, None]) * freq[None, None, :] % bins
    cosines = np.cos(phase * (2.0 * math.pi / bins))
    return np.einsum("ot,fgt->ofg", weights, cosines) / bins


def pair_of(step, core, blocks):
    half = blocks // 2
    main = half * half
    tail = step // main
    row = (step // half) * (1 - tail) + (step - main) * tail
    return core * (half - half // 2 * tail) + row, (step % half) * (1 - tail) + half * tail


def tile_kernel(bins, groups, rec, here, blocks, shift, xa_ref, xb_ref, kmat_ref,
                out_ref, left, gram, tile, mirror, local_sem, send_sem, recv_sem):
    step = pl.program_id(0)
    count = pl.num_programs(0) - 1
    tm = lax.axis_index("tm")
    core = lax.rem(tm, 2)
    partner = tm + 1 - 2 * core
    half = blocks // 2
    deep = groups * 2 * rec
    slot = lax.rem(step, 2)
    a, d = pair_of(jnp.minimum(step, count - 1), core, blocks)
    b = lax.rem(a + d, blocks)

    def copies(at, kind):
        ta, td = pair_of(at, core, blocks)
        tb = lax.rem(ta + td, blocks)
        where = lax.rem(at, 2)
        first, second = (ta, tb) if kind == 0 else (tb, ta)
        rows = pl.ds(pl.multiple_of(first * BLOCK, BLOCK), BLOCK)
        cols = pl.ds(pl.multiple_of(second * BLOCK, BLOCK), BLOCK)
        held = tile if kind == 0 else mirror
        kept = pltpu.make_async_copy(
            held.at[where, pl.ds(core * here, here)], out_ref.at[:, :, rows, cols],
            local_sem.at[kind, where],
        )
        given = pltpu.make_async_remote_copy(
            src_ref=held.at[where, pl.ds((1 - core) * here, here)],
            dst_ref=out_ref.at[:, :, rows, cols],
            send_sem=send_sem.at[kind, where],
            recv_sem=recv_sem.at[kind, at],
            device_id={"tm": partner},
            device_id_type=pl.DeviceIdType.MESH,
        )
        return kept, given

    def begin(at, kind):
        kept, given = copies(at, kind)
        kept.start()
        given.start()

    def finish(at, kind):
        kept, given = copies(at, kind)
        kept.wait()
        given.wait_send()

    def turned(at):
        return pair_of(at, core, blocks)[1] > 0

    @pl.when(step == 0)
    def _():
        barrier = pltpu.get_barrier_semaphore()
        pl.semaphore_signal(
            barrier, inc=1, device_id={"tm": partner}, device_id_type=pl.DeviceIdType.MESH
        )
        pl.semaphore_wait(barrier, 1)

    @pl.when((step < count) & ((d == 0) | (step >= half * half)))
    def _():
        @pl.loop(0, bins)
        def _(g):
            block = xa_ref[:, 0, g]
            crossed = jnp.concatenate([-block[:, rec:], block[:, :rec]], axis=1)
            left[g, :BLOCK] = block.reshape(deep, BLOCK).T
            left[g, BLOCK:] = crossed.reshape(deep, BLOCK).T

    before = jnp.maximum(step - 1, 0)
    old = lax.rem(step + 1, 2)

    @pl.when(step >= 3)
    def _():
        @pl.when(turned(step - 3))
        def _():
            finish(step - 3, 1)

    def gram_of(g):
        both = jnp.dot(
            left[g], xb_ref[:, 0, g].reshape(deep, BLOCK), preferred_element_type=jnp.float32
        ).astype(jnp.bfloat16)
        gram[0, g] = both[:BLOCK]
        gram[1, g] = both[BLOCK:]

    def turn(f):
        mirror[old, f, 0] = tile[old, f, 0].T
        mirror[old, f, 1] = -tile[old, f, 1].T

    per = bins // (2 * here)

    @pl.when(step < count)
    def _():
        @pl.loop(0, 2 * here)
        def _(f):
            for k in range(per):
                gram_of(f * per + k)
            turn(f)

    @pl.when(step == count)
    def _():
        @pl.loop(0, 2 * here)
        def _(f):
            turn(f)

    @pl.when(step >= 1)
    def _():
        @pl.when(turned(before))
        def _():
            begin(before, 1)

    @pl.when(step >= 2)
    def _():
        finish(step - 2, 0)

    @pl.when(step < count)
    def _():
        kernel = kmat_ref[shift[a * blocks + b]]

        @pl.loop(0, BLOCK // SUB // 4)
        def _(quad):
            for k in range(4):
                rows = pl.ds(pl.multiple_of((quad * 4 + k) * SUB, SUB), SUB)
                for c in range(2):
                    part = gram[c, :, rows, :].reshape(bins * SUB, BLOCK)
                    mixed = jnp.dot(kernel, part, preferred_element_type=jnp.float32)
                    tile[slot, :, c, rows, :] = mixed.astype(jnp.bfloat16).reshape(
                        2 * here, SUB, BLOCK
                    )

        begin(step, 0)

    @pl.when(step == count)
    def _():
        finish(count - 1, 0)
        for at in (count - 2, count - 1):
            @pl.when(turned(at))
            def _():
                finish(at, 1)

        @pl.loop(0, count)
        def _(at):
            copies(at, 0)[1].wait_recv()

            @pl.when(turned(at))
            def _():
                copies(at, 1)[1].wait_recv()


def windowed_tiles(spectra, shift, kmat, stations):
    groups, bands, bins, both, width = spectra.shape
    rec = both // 2
    here = bins // groups
    per = width // BLOCK
    blocks = stations // BLOCK
    count = blocks * (blocks + 1) // 4
    block = (groups, 1, bins, both, BLOCK)
    flops = count * bins * 2 * BLOCK * BLOCK * (groups * both * 2 + 4 * here * SUB)

    def pick_a(s, sh):
        a, _ = pair_of(jnp.minimum(s, count - 1), lax.rem(lax.axis_index("tm"), 2), blocks)
        return (0, a // per, 0, 0, lax.rem(a, per))

    def pick_b(s, sh):
        a, d = pair_of(jnp.minimum(s, count - 1), lax.rem(lax.axis_index("tm"), 2), blocks)
        b = lax.rem(a + d, blocks)
        return (0, b // per, 0, 0, lax.rem(b, per))

    return pl.pallas_call(
        functools.partial(tile_kernel, bins, groups, rec, here, blocks),
        out_shape=jax.ShapeDtypeStruct((here, 2, stations, stations), jnp.bfloat16),
        grid_spec=pltpu.PrefetchScalarGridSpec(
            num_scalar_prefetch=1,
            grid=(count + 1,),
            in_specs=[
                pl.BlockSpec(block, pick_a),
                pl.BlockSpec(block, pick_b),
                pl.BlockSpec(kmat.shape, lambda s, sh: (0, 0, 0)),
            ],
            out_specs=pl.BlockSpec(memory_space=pl.ANY),
            scratch_shapes=[
                pltpu.VMEM((bins, 2 * BLOCK, groups * both), jnp.bfloat16),
                pltpu.VMEM((2, bins, BLOCK, BLOCK), jnp.bfloat16),
                pltpu.VMEM((2, 2 * here, 2, BLOCK, BLOCK), jnp.bfloat16),
                pltpu.VMEM((2, 2 * here, 2, BLOCK, BLOCK), jnp.bfloat16),
                pltpu.SemaphoreType.DMA((2, 2)),
                pltpu.SemaphoreType.DMA((2, 2)),
                pltpu.SemaphoreType.DMA((2, count)),
            ],
        ),
        compiler_params=pltpu.CompilerParams(
            vmem_limit_bytes=60 * 2**20, collective_id=0, has_side_effects=True
        ),
        cost_estimate=pl.CostEstimate(flops=flops, bytes_accessed=200 * 2**20, transcendentals=0),
        name="windowed_tiles",
    )(shift, spectra, spectra, kmat)


def square_kernel(scale, place, rows_ref, cols_ref, out_ref):
    left_re = rows_ref[0, 0]
    left_im = rows_ref[0, 1]
    right_re = cols_ref[0, 0]
    right_im = cols_ref[0, 1]
    dot = functools.partial(jnp.dot, preferred_element_type=jnp.float32)
    squares = dot(left_re, right_re)
    crosses = dot(left_im, right_im)
    both = dot(left_re + left_im, right_re + right_im)
    out_ref[0, 0] = ((squares - crosses) * scale).astype(jnp.bfloat16)
    out_ref[1, 0] = ((both - squares - crosses) * scale).astype(jnp.bfloat16)


def square_tiles(windowed, place, tile_rows, tile_cols, scale):
    here, _, stations, _ = windowed.shape
    wide = min(512, tile_cols)
    count = tile_cols // wide
    return pl.pallas_call(
        functools.partial(square_kernel, scale),
        out_shape=jax.ShapeDtypeStruct((2, here, tile_rows, tile_cols), jnp.bfloat16),
        grid_spec=pltpu.PrefetchScalarGridSpec(
            num_scalar_prefetch=1,
            grid=(here, count),
            in_specs=[
                pl.BlockSpec((1, 2, tile_rows, stations), lambda f, j, p: (f, 0, p[0], 0)),
                pl.BlockSpec((1, 2, stations, wide), lambda f, j, p: (f, 0, 0, p[1] * count + j)),
            ],
            out_specs=pl.BlockSpec((2, 1, tile_rows, wide), lambda f, j, p: (0, f, 0, j)),
        ),
        compiler_params=pltpu.CompilerParams(vmem_limit_bytes=56 * 2**20),
        cost_estimate=pl.CostEstimate(
            flops=8 * here * tile_rows * tile_cols * stations,
            bytes_accessed=60 * 2**20,
            transcendentals=0,
        ),
        name="square_tiles",
    )(place, windowed, windowed)


def on_device(mesh, records, offsets):
    rec, _, bins, width = records.shape
    groups = mesh.shape["tm"]
    bands = mesh.shape["row"]
    stations = width * bands * mesh.shape["col"]
    here = bins // groups
    own = jnp.transpose(records, (2, 1, 0, 3)).reshape(bins, 2 * rec, width)
    band = lax.all_gather(own, "col", axis=2, tiled=True)
    spectra = lax.all_gather(band, ("tm", "row"), axis=0)
    spectra = spectra.reshape(groups, bands, bins, 2 * rec, stations // bands)

    chip = lax.axis_index("tm") // 2
    mine = lax.dynamic_slice_in_dim(
        jnp.asarray(lag_table(bins).astype(np.float32)), chip * 2 * here, 2 * here, 1
    )
    kmat = mine[:, :, None, :, None] * jnp.eye(SUB, dtype=jnp.float32)[None, None, :, None, :]
    kmat = kmat.reshape(NOFF, 2 * here * SUB, bins * SUB).astype(jnp.bfloat16)
    shift = ((offsets + offsets.T) % NOFF).reshape(-1)
    windowed = windowed_tiles(spectra, shift, kmat, stations)
    place = jnp.stack([lax.axis_index("row"), lax.axis_index("col")]).astype(jnp.int32)
    scale = 1.0 / (rec * groups * math.sqrt(stations))
    return square_tiles(
        windowed, place, stations // bands, stations // mesh.shape["col"], scale
    )


def solution(mesh):
    return jax.shard_map(
        functools.partial(on_device, mesh),
        mesh=mesh,
        in_specs=(P("tm", None, None, ("row", "col")), P()),
        out_specs=P(None, "tm", "row", "col"),
        check_vma=False,
    )
```

```python
import functools
import math

import jax
import jax.numpy as jnp
import numpy as np
from jax import lax
from jax.experimental import pallas as pl
from jax.experimental.pallas import tpu as pltpu
from jax.sharding import PartitionSpec as P

BLOCK = 256
NOFF = 4
SUB = 16


def lag_table(bins):
    freq = np.arange(bins)
    lag = np.minimum(freq, bins - freq)
    starts = np.arange(NOFF)[:, None] + 2
    inside = (lag[None, :] >= starts) & (lag[None, :] < starts + 3)
    weights = np.where(inside, 1.0, 0.1)
    phase = (freq[:, None, None] - freq[None, :, None]) * freq[None, None, :] % bins
    cosines = np.cos(phase * (2.0 * math.pi / bins))
    return np.einsum("ot,fgt->ofg", weights, cosines) / bins


def gather_kernel(groups, bands, cols, own_ref, out_ref, local_sem, send_sem, recv_sem):
    tm = lax.axis_index("tm")
    row = lax.axis_index("row")
    col = lax.axis_index("col")
    core = lax.rem(tm, 2)
    partner = tm + 1 - 2 * core
    both = own_ref.shape[0]
    half = both // 2
    bits = (bands - 1).bit_length()

    def other_row(k):
        total = 0
        for bit in range(bits):
            own_bit = lax.rem(row // 2**bit, 2)
            total = total + 2**bit * lax.rem(own_bit + k // 2**bit % 2, 2)
        return total

    chips = [lax.rem(tm + 2 * k, groups) for k in range(1, groups // 2)]
    columns = [lax.rem(col + k, cols) for k in range(1, cols)]
    rows = [other_row(k) for k in range(1, bands)]

    barrier = pltpu.get_barrier_semaphore()
    friends = (
        [{"tm": t} for t in chips] + [{"col": q} for q in columns]
        + [{"row": r} for r in rows] + [{"tm": partner}]
    )
    for friend in friends:
        pl.semaphore_signal(
            barrier, inc=1, device_id=friend, device_id_type=pl.DeviceIdType.MESH
        )
    pl.semaphore_wait(barrier, len(friends))

    started = []

    def place(t, r, q):
        return out_ref.at[t, r * cols + q]

    def copy(t, r, q, target, part, source=None):
        source = place(t, r, q) if source is None else source
        target_ref = place(t, r, q)
        if part is not None:
            source = source.at[pl.ds(part * half, half)]
            target_ref = target_ref.at[pl.ds(part * half, half)]
        return pltpu.make_async_remote_copy(
            src_ref=source, dst_ref=target_ref,
            send_sem=send_sem.at[len(started)],
            recv_sem=recv_sem.at[part or 0, t, r * cols + q],
            device_id=target, device_id_type=pl.DeviceIdType.MESH,
        )

    def send(t, r, q, target, part=None, source=None):
        one = copy(t, r, q, target, part, source)
        one.start()
        started.append(one)

    def arrive(t, r, q, part=None):
        piece = place(t, r, q)
        if part is not None:
            piece = piece.at[pl.ds(part * half, half)]
        pltpu.make_async_copy(piece, piece, recv_sem.at[part or 0, t, r * cols + q]).wait()

    def spread(r, source=None):
        for t in chips:
            send(tm, r, col, {"tm": t}, source=source)
        for q in columns:
            send(tm, r, col, {"col": q}, source=source)
        send(tm, r, col, {"tm": partner}, source=source)

    def pass_on(r):
        for t in chips:
            arrive(t, r, col)
            for q in columns:
                send(t, r, col, {"col": q}, 0)
            send(t, r, col, {"tm": partner})
        for q in columns:
            arrive(tm, r, q)
            for t in chips:
                send(tm, r, q, {"tm": t}, 1)
            send(tm, r, q, {"tm": partner})

    mine = pltpu.make_async_copy(own_ref, place(tm, row, col), local_sem)
    mine.start()
    for r in rows:
        send(tm, row, col, {"row": r}, source=own_ref)
    spread(row, own_ref)
    waiting = [row]
    for r in rows:
        arrive(tm, r, col)
        spread(r)
        pass_on(waiting.pop())
        waiting.append(r)
    pass_on(waiting.pop())
    for r in [row] + rows:
        for t in chips:
            for q in columns:
                arrive(t, r, q, 0)
                arrive(t, r, q, 1)
                send(t, r, q, {"tm": partner})
    for chip in range(groups // 2):
        t = lax.rem(partner + 2 * chip, groups)
        for k in range(bands * cols):
            arrive(t, k // cols, k % cols)
    mine.wait()
    for one in started:
        one.wait_send()


def gather_pieces(own, groups, bands, cols):
    chips = groups // 2
    sends = (bands - 1) + bands * (chips - 1 + cols - 1 + 1)
    sends += bands * ((chips - 1) * cols + (cols - 1) * chips + (chips - 1) * (cols - 1))
    return pl.pallas_call(
        functools.partial(gather_kernel, groups, bands, cols),
        out_shape=jax.ShapeDtypeStruct((groups, bands * cols) + own.shape, own.dtype),
        in_specs=[pl.BlockSpec(memory_space=pl.ANY)],
        out_specs=pl.BlockSpec(memory_space=pl.ANY),
        scratch_shapes=[
            pltpu.SemaphoreType.DMA,
            pltpu.SemaphoreType.DMA((sends,)),
            pltpu.SemaphoreType.DMA((2, groups, bands * cols)),
        ],
        compiler_params=pltpu.CompilerParams(collective_id=1, has_side_effects=True),
        cost_estimate=pl.CostEstimate(flops=0, bytes_accessed=50 * 2**20, transcendentals=0),
        name="gather_pieces",
    )(own)


def pair_of(step, core, blocks):
    half = blocks // 2
    main = half * half
    tail = step // main
    row = (step // half) * (1 - tail) + (step - main) * tail
    return core * (half - half // 2 * tail) + row, (step % half) * (1 - tail) + half * tail


def tile_kernel(bins, groups, rec, here, blocks, shift, xa_ref, xb_ref, kmat_ref,
                out_ref, left, gram, tile, mirror, local_sem, send_sem, recv_sem):
    step = pl.program_id(0)
    count = pl.num_programs(0) - 1
    tm = lax.axis_index("tm")
    core = lax.rem(tm, 2)
    partner = tm + 1 - 2 * core
    half = blocks // 2
    deep = groups * 2 * rec
    slot = lax.rem(step, 2)
    a, d = pair_of(jnp.minimum(step, count - 1), core, blocks)
    b = lax.rem(a + d, blocks)

    def copies(at, kind):
        ta, td = pair_of(at, core, blocks)
        tb = lax.rem(ta + td, blocks)
        where = lax.rem(at, 2)
        first, second = (ta, tb) if kind == 0 else (tb, ta)
        rows = pl.ds(pl.multiple_of(first * BLOCK, BLOCK), BLOCK)
        cols = pl.ds(pl.multiple_of(second * BLOCK, BLOCK), BLOCK)
        held = tile if kind == 0 else mirror
        kept = pltpu.make_async_copy(
            held.at[where, pl.ds(core * here, here)], out_ref.at[:, :, rows, cols],
            local_sem.at[kind, where],
        )
        given = pltpu.make_async_remote_copy(
            src_ref=held.at[where, pl.ds((1 - core) * here, here)],
            dst_ref=out_ref.at[:, :, rows, cols],
            send_sem=send_sem.at[kind, where],
            recv_sem=recv_sem.at[kind, at],
            device_id={"tm": partner},
            device_id_type=pl.DeviceIdType.MESH,
        )
        return kept, given

    def begin(at, kind):
        kept, given = copies(at, kind)
        kept.start()
        given.start()

    def finish(at, kind):
        kept, given = copies(at, kind)
        kept.wait()
        given.wait_send()

    def turned(at):
        return pair_of(at, core, blocks)[1] > 0

    @pl.when(step == 0)
    def _():
        barrier = pltpu.get_barrier_semaphore()
        pl.semaphore_signal(
            barrier, inc=1, device_id={"tm": partner}, device_id_type=pl.DeviceIdType.MESH
        )
        pl.semaphore_wait(barrier, 1)

    @pl.when((step < count) & ((d == 0) | (step >= half * half)))
    def _():
        @pl.loop(0, bins)
        def _(g):
            block = xa_ref[:, 0, g]
            crossed = jnp.concatenate([-block[:, rec:], block[:, :rec]], axis=1)
            left[g, :BLOCK] = block.reshape(deep, BLOCK).T
            left[g, BLOCK:] = crossed.reshape(deep, BLOCK).T

    before = jnp.maximum(step - 1, 0)
    old = lax.rem(step + 1, 2)

    @pl.when(step >= 3)
    def _():
        @pl.when(turned(step - 3))
        def _():
            finish(step - 3, 1)

    def gram_of(g):
        both = jnp.dot(
            left[g], xb_ref[:, 0, g].reshape(deep, BLOCK), preferred_element_type=jnp.float32
        ).astype(jnp.bfloat16)
        gram[0, g] = both[:BLOCK]
        gram[1, g] = both[BLOCK:]

    def turn(f):
        mirror[old, f, 0] = tile[old, f, 0].T
        mirror[old, f, 1] = -tile[old, f, 1].T

    per = bins // (2 * here)

    @pl.when(step < count)
    def _():
        @pl.loop(0, 2 * here)
        def _(f):
            for k in range(per):
                gram_of(f * per + k)
            turn(f)

    @pl.when(step == count)
    def _():
        @pl.loop(0, 2 * here)
        def _(f):
            turn(f)

    @pl.when(step >= 1)
    def _():
        @pl.when(turned(before))
        def _():
            begin(before, 1)

    @pl.when(step >= 2)
    def _():
        finish(step - 2, 0)

    @pl.when(step < count)
    def _():
        kernel = kmat_ref[shift[a * blocks + b]]

        @pl.loop(0, BLOCK // SUB // 4)
        def _(quad):
            for k in range(4):
                rows = pl.ds(pl.multiple_of((quad * 4 + k) * SUB, SUB), SUB)
                for c in range(2):
                    part = gram[c, :, rows, :].reshape(bins * SUB, BLOCK)
                    mixed = jnp.dot(kernel, part, preferred_element_type=jnp.float32)
                    tile[slot, :, c, rows, :] = mixed.astype(jnp.bfloat16).reshape(
                        2 * here, SUB, BLOCK
                    )

        begin(step, 0)

    @pl.when(step == count)
    def _():
        finish(count - 1, 0)
        for at in (count - 2, count - 1):
            @pl.when(turned(at))
            def _():
                finish(at, 1)

        @pl.loop(0, count)
        def _(at):
            copies(at, 0)[1].wait_recv()

            @pl.when(turned(at))
            def _():
                copies(at, 1)[1].wait_recv()


def windowed_tiles(spectra, shift, kmat, stations):
    groups, bands, bins, both, width = spectra.shape
    rec = both // 2
    here = bins // groups
    per = width // BLOCK
    blocks = stations // BLOCK
    count = blocks * (blocks + 1) // 4
    block = (groups, 1, bins, both, BLOCK)
    flops = count * bins * 2 * BLOCK * BLOCK * (groups * both * 2 + 4 * here * SUB)

    def pick_a(s, sh):
        a, _ = pair_of(jnp.minimum(s, count - 1), lax.rem(lax.axis_index("tm"), 2), blocks)
        return (0, a // per, 0, 0, lax.rem(a, per))

    def pick_b(s, sh):
        a, d = pair_of(jnp.minimum(s, count - 1), lax.rem(lax.axis_index("tm"), 2), blocks)
        b = lax.rem(a + d, blocks)
        return (0, b // per, 0, 0, lax.rem(b, per))

    return pl.pallas_call(
        functools.partial(tile_kernel, bins, groups, rec, here, blocks),
        out_shape=jax.ShapeDtypeStruct((here, 2, stations, stations), jnp.bfloat16),
        grid_spec=pltpu.PrefetchScalarGridSpec(
            num_scalar_prefetch=1,
            grid=(count + 1,),
            in_specs=[
                pl.BlockSpec(block, pick_a),
                pl.BlockSpec(block, pick_b),
                pl.BlockSpec(kmat.shape, lambda s, sh: (0, 0, 0)),
            ],
            out_specs=pl.BlockSpec(memory_space=pl.ANY),
            scratch_shapes=[
                pltpu.VMEM((bins, 2 * BLOCK, groups * both), jnp.bfloat16),
                pltpu.VMEM((2, bins, BLOCK, BLOCK), jnp.bfloat16),
                pltpu.VMEM((2, 2 * here, 2, BLOCK, BLOCK), jnp.bfloat16),
                pltpu.VMEM((2, 2 * here, 2, BLOCK, BLOCK), jnp.bfloat16),
                pltpu.SemaphoreType.DMA((2, 2)),
                pltpu.SemaphoreType.DMA((2, 2)),
                pltpu.SemaphoreType.DMA((2, count)),
            ],
        ),
        compiler_params=pltpu.CompilerParams(
            vmem_limit_bytes=60 * 2**20, collective_id=0, has_side_effects=True
        ),
        cost_estimate=pl.CostEstimate(flops=flops, bytes_accessed=200 * 2**20, transcendentals=0),
        name="windowed_tiles",
    )(shift, spectra, spectra, kmat)


def square_kernel(scale, place, rows_ref, cols_ref, out_ref):
    left_re = rows_ref[0, 0]
    left_im = rows_ref[0, 1]
    right_re = cols_ref[0, 0]
    right_im = cols_ref[0, 1]
    dot = functools.partial(jnp.dot, preferred_element_type=jnp.float32)
    squares = dot(left_re, right_re)
    crosses = dot(left_im, right_im)
    both = dot(left_re + left_im, right_re + right_im)
    out_ref[0, 0] = ((squares - crosses) * scale).astype(jnp.bfloat16)
    out_ref[1, 0] = ((both - squares - crosses) * scale).astype(jnp.bfloat16)


def square_tiles(windowed, place, tile_rows, tile_cols, scale):
    here, _, stations, _ = windowed.shape
    wide = min(512, tile_cols)
    count = tile_cols // wide
    return pl.pallas_call(
        functools.partial(square_kernel, scale),
        out_shape=jax.ShapeDtypeStruct((2, here, tile_rows, tile_cols), jnp.bfloat16),
        grid_spec=pltpu.PrefetchScalarGridSpec(
            num_scalar_prefetch=1,
            grid=(here, count),
            in_specs=[
                pl.BlockSpec((1, 2, tile_rows, stations), lambda f, j, p: (f, 0, p[0], 0)),
                pl.BlockSpec((1, 2, stations, wide), lambda f, j, p: (f, 0, 0, p[1] * count + j)),
            ],
            out_specs=pl.BlockSpec((2, 1, tile_rows, wide), lambda f, j, p: (0, f, 0, j)),
        ),
        compiler_params=pltpu.CompilerParams(vmem_limit_bytes=56 * 2**20),
        cost_estimate=pl.CostEstimate(
            flops=8 * here * tile_rows * tile_cols * stations,
            bytes_accessed=60 * 2**20,
            transcendentals=0,
        ),
        name="square_tiles",
    )(place, windowed, windowed)


def on_device(mesh, records, offsets):
    rec, _, bins, width = records.shape
    groups = mesh.shape["tm"]
    bands = mesh.shape["row"]
    stations = width * bands * mesh.shape["col"]
    here = bins // groups
    own = jnp.transpose(records, (2, 1, 0, 3)).reshape(bins, 2 * rec, width)
    if width == BLOCK:
        spectra = gather_pieces(own, groups, bands, mesh.shape["col"])
    else:
        band = lax.all_gather(own, "col", axis=2, tiled=True)
        spectra = lax.all_gather(band, ("tm", "row"), axis=0)
        spectra = spectra.reshape(groups, bands, bins, 2 * rec, stations // bands)

    chip = lax.axis_index("tm") // 2
    mine = lax.dynamic_slice_in_dim(
        jnp.asarray(lag_table(bins).astype(np.float32)), chip * 2 * here, 2 * here, 1
    )
    kmat = mine[:, :, None, :, None] * jnp.eye(SUB, dtype=jnp.float32)[None, None, :, None, :]
    kmat = kmat.reshape(NOFF, 2 * here * SUB, bins * SUB).astype(jnp.bfloat16)
    shift = ((offsets + offsets.T) % NOFF).reshape(-1)
    windowed = windowed_tiles(spectra, shift, kmat, stations)
    place = jnp.stack([lax.axis_index("row"), lax.axis_index("col")]).astype(jnp.int32)
    scale = 1.0 / (rec * groups * math.sqrt(stations))
    return square_tiles(
        windowed, place, stations // bands, stations // mesh.shape["col"], scale
    )


def solution(mesh):
    return jax.shard_map(
        functools.partial(on_device, mesh),
        mesh=mesh,
        in_specs=(P("tm", None, None, ("row", "col")), P()),
        out_specs=P(None, "tm", "row", "col"),
        check_vma=False,
    )
```

```python
import functools
import math

import jax
import jax.numpy as jnp
import numpy as np
from jax import lax
from jax.experimental import pallas as pl
from jax.experimental.pallas import tpu as pltpu
from jax.sharding import PartitionSpec as P

BLOCK = 256
NOFF = 4
SUB = 16


def lag_table(bins):
    freq = np.arange(bins)
    lag = np.minimum(freq, bins - freq)
    starts = np.arange(NOFF)[:, None] + 2
    inside = (lag[None, :] >= starts) & (lag[None, :] < starts + 3)
    weights = np.where(inside, 1.0, 0.1)
    phase = (freq[:, None, None] - freq[None, :, None]) * freq[None, None, :] % bins
    cosines = np.cos(phase * (2.0 * math.pi / bins))
    return np.einsum("ot,fgt->ofg", weights, cosines) / bins


def pair_of(step, core, blocks):
    half = blocks // 2
    main = half * half
    tail = step // main
    row = (step // half) * (1 - tail) + (step - main) * tail
    return core * (half - half // 2 * tail) + row, (step % half) * (1 - tail) + half * tail


def tile_kernel(bins, groups, rec, here, blocks, shift, xa_ref, xb_ref, kmat_ref,
                out_ref, left, gram, tile, mirror, local_sem, send_sem, recv_sem):
    step = pl.program_id(0)
    count = pl.num_programs(0) - 1
    tm = lax.axis_index("tm")
    core = lax.rem(tm, 2)
    partner = tm + 1 - 2 * core
    half = blocks // 2
    deep = groups * 2 * rec
    slot = lax.rem(step, 2)
    a, d = pair_of(jnp.minimum(step, count - 1), core, blocks)
    b = lax.rem(a + d, blocks)

    def copies(at, kind):
        ta, td = pair_of(at, core, blocks)
        tb = lax.rem(ta + td, blocks)
        where = lax.rem(at, 2)
        first, second = (ta, tb) if kind == 0 else (tb, ta)
        rows = pl.ds(pl.multiple_of(first * BLOCK, BLOCK), BLOCK)
        cols = pl.ds(pl.multiple_of(second * BLOCK, BLOCK), BLOCK)
        held = tile if kind == 0 else mirror
        kept = pltpu.make_async_copy(
            held.at[where, pl.ds(core * here, here)], out_ref.at[:, :, rows, cols],
            local_sem.at[kind, where],
        )
        given = pltpu.make_async_remote_copy(
            src_ref=held.at[where, pl.ds((1 - core) * here, here)],
            dst_ref=out_ref.at[:, :, rows, cols],
            send_sem=send_sem.at[kind, where],
            recv_sem=recv_sem.at[kind, at],
            device_id={"tm": partner},
            device_id_type=pl.DeviceIdType.MESH,
        )
        return kept, given

    def begin(at, kind):
        kept, given = copies(at, kind)
        kept.start()
        given.start()

    def finish(at, kind):
        kept, given = copies(at, kind)
        kept.wait()
        given.wait_send()

    def turned(at):
        return pair_of(at, core, blocks)[1] > 0

    @pl.when(step == 0)
    def _():
        barrier = pltpu.get_barrier_semaphore()
        pl.semaphore_signal(
            barrier, inc=1, device_id={"tm": partner}, device_id_type=pl.DeviceIdType.MESH
        )
        pl.semaphore_wait(barrier, 1)

    @pl.when((step < count) & ((d == 0) | (step >= half * half)))
    def _():
        @pl.loop(0, bins)
        def _(g):
            block = xa_ref[:, 0, g]
            crossed = jnp.concatenate([-block[:, rec:], block[:, :rec]], axis=1)
            left[g, :BLOCK] = block.reshape(deep, BLOCK).T
            left[g, BLOCK:] = crossed.reshape(deep, BLOCK).T

    before = jnp.maximum(step - 1, 0)
    old = lax.rem(step + 1, 2)

    @pl.when(step >= 3)
    def _():
        @pl.when(turned(step - 3))
        def _():
            finish(step - 3, 1)

    def gram_of(g):
        both = jnp.dot(
            left[g], xb_ref[:, 0, g].reshape(deep, BLOCK), preferred_element_type=jnp.float32
        ).astype(jnp.bfloat16)
        gram[0, g] = both[:BLOCK]
        gram[1, g] = both[BLOCK:]

    def turn(f):
        mirror[old, f, 0] = tile[old, f, 0].T
        mirror[old, f, 1] = -tile[old, f, 1].T

    per = bins // (2 * here)

    @pl.when(step < count)
    def _():
        @pl.loop(0, 2 * here)
        def _(f):
            for k in range(per):
                gram_of(f * per + k)
            turn(f)

    @pl.when(step == count)
    def _():
        @pl.loop(0, 2 * here)
        def _(f):
            turn(f)

    @pl.when(step >= 1)
    def _():
        @pl.when(turned(before))
        def _():
            begin(before, 1)

    @pl.when(step >= 2)
    def _():
        finish(step - 2, 0)

    @pl.when(step < count)
    def _():
        kernel = kmat_ref[shift[a * blocks + b]]

        @pl.loop(0, BLOCK // SUB // 4)
        def _(quad):
            for k in range(4):
                rows = pl.ds(pl.multiple_of((quad * 4 + k) * SUB, SUB), SUB)
                for c in range(2):
                    part = gram[c, :, rows, :].reshape(bins * SUB, BLOCK)
                    mixed = jnp.dot(kernel, part, preferred_element_type=jnp.float32)
                    tile[slot, :, c, rows, :] = mixed.astype(jnp.bfloat16).reshape(
                        2 * here, SUB, BLOCK
                    )

        begin(step, 0)

    @pl.when(step == count)
    def _():
        finish(count - 1, 0)
        for at in (count - 2, count - 1):
            @pl.when(turned(at))
            def _():
                finish(at, 1)

        @pl.loop(0, count)
        def _(at):
            copies(at, 0)[1].wait_recv()

            @pl.when(turned(at))
            def _():
                copies(at, 1)[1].wait_recv()


def windowed_tiles(spectra, shift, kmat, stations):
    groups, bands, bins, both, width = spectra.shape
    rec = both // 2
    here = bins // groups
    per = width // BLOCK
    blocks = stations // BLOCK
    count = blocks * (blocks + 1) // 4
    block = (groups, 1, bins, both, BLOCK)
    flops = count * bins * 2 * BLOCK * BLOCK * (groups * both * 2 + 4 * here * SUB)

    def pick_a(s, sh):
        a, _ = pair_of(jnp.minimum(s, count - 1), lax.rem(lax.axis_index("tm"), 2), blocks)
        return (0, a // per, 0, 0, lax.rem(a, per))

    def pick_b(s, sh):
        a, d = pair_of(jnp.minimum(s, count - 1), lax.rem(lax.axis_index("tm"), 2), blocks)
        b = lax.rem(a + d, blocks)
        return (0, b // per, 0, 0, lax.rem(b, per))

    return pl.pallas_call(
        functools.partial(tile_kernel, bins, groups, rec, here, blocks),
        out_shape=jax.ShapeDtypeStruct((here, 2, stations, stations), jnp.bfloat16),
        grid_spec=pltpu.PrefetchScalarGridSpec(
            num_scalar_prefetch=1,
            grid=(count + 1,),
            in_specs=[
                pl.BlockSpec(block, pick_a),
                pl.BlockSpec(block, pick_b),
                pl.BlockSpec(kmat.shape, lambda s, sh: (0, 0, 0)),
            ],
            out_specs=pl.BlockSpec(memory_space=pl.ANY),
            scratch_shapes=[
                pltpu.VMEM((bins, 2 * BLOCK, groups * both), jnp.bfloat16),
                pltpu.VMEM((2, bins, BLOCK, BLOCK), jnp.bfloat16),
                pltpu.VMEM((2, 2 * here, 2, BLOCK, BLOCK), jnp.bfloat16),
                pltpu.VMEM((2, 2 * here, 2, BLOCK, BLOCK), jnp.bfloat16),
                pltpu.SemaphoreType.DMA((2, 2)),
                pltpu.SemaphoreType.DMA((2, 2)),
                pltpu.SemaphoreType.DMA((2, count)),
            ],
        ),
        compiler_params=pltpu.CompilerParams(
            vmem_limit_bytes=60 * 2**20, collective_id=0, has_side_effects=True
        ),
        cost_estimate=pl.CostEstimate(flops=flops, bytes_accessed=200 * 2**20, transcendentals=0),
        name="windowed_tiles",
    )(shift, spectra, spectra, kmat)


def fused_kernel(groups, bands, cols, bins, rec, here, shift, own_ref, kmat_ref, out_ref,
                 held, left, gram, tile, mirror, own_sem, piece_send, piece_recv,
                 local_sem, send_sem, recv_sem):
    step = pl.program_id(0)
    count = pl.num_programs(0) - 1
    tm = lax.axis_index("tm")
    row = lax.axis_index("row")
    col = lax.axis_index("col")
    core = lax.rem(tm, 2)
    partner = tm + 1 - 2 * core
    blocks = bands * cols
    deep = groups * 2 * rec
    slot = lax.rem(step, 2)
    old = lax.rem(step + 1, 2)
    mesh_id = pl.DeviceIdType.MESH
    chip = lax.rem(tm + 2, groups)
    side = lax.rem(col + 1, cols)
    bin_half = bins // 2
    arrival = [(0, 0), (1, 0), (0, 1), (2, 0), (1, 1), (3, 0), (2, 1), (3, 1)]

    def row_at(k):
        low = lax.rem(lax.rem(row, 2) + k % 2, 2)
        high = lax.rem(row // 2 + k // 2, 2)
        return 2 * high + low

    def block_at(n):
        total = 0
        for index, (k, other) in enumerate(arrival):
            where = row_at(k) * cols + (side if other else col)
            total = total + jnp.where(n == index, where, 0)
        return total

    def pair(at, who):
        t = 2 * at + who
        n = 0
        for index in range(1, blocks):
            n = n + jnp.minimum(t // (index * (index + 1) // 2), 1)
        return n, t - n * (n + 1) // 2

    def send(index, t, k, q, target, part=None, source=None):
        block = row_at(k) * cols + q
        there = held.at[t, block]
        source = there if source is None else source
        if part is not None:
            source = source.at[pl.ds(part * bin_half, bin_half)]
            there = there.at[pl.ds(part * bin_half, bin_half)]
        return pltpu.make_async_remote_copy(
            src_ref=source, dst_ref=there, send_sem=piece_send.at[index],
            recv_sem=piece_recv.at[part or 0, t, block], device_id=target, device_id_type=mesh_id,
        )

    def arrive(t, k, q, part=None):
        block = row_at(k) * cols + q
        piece = held.at[t, block]
        if part is not None:
            piece = piece.at[pl.ds(part * bin_half, bin_half)]
        pltpu.make_async_copy(piece, piece, piece_recv.at[part or 0, t, block]).wait()

    def own_sends():
        return [send(k - 1, tm, 0, col, {"row": row_at(k)}, source=own_ref) for k in (1, 2, 3)]

    def spread(k):
        source = own_ref if k == 0 else None
        base = 3 + 8 * k
        return [
            send(base, tm, k, col, {"tm": chip}, source=source),
            send(base + 1, tm, k, col, {"col": side}, source=source),
            send(base + 2, tm, k, col, {"tm": partner}, source=source),
        ]

    def pass_chip(k):
        base = 6 + 8 * k
        return [
            send(base, chip, k, col, {"col": side}, 0),
            send(base + 1, chip, k, col, {"tm": partner}),
        ]

    def pass_side(k):
        base = 8 + 8 * k
        return [
            send(base, tm, k, side, {"tm": chip}, 1),
            send(base + 1, tm, k, side, {"tm": partner}),
        ]

    def pass_corner(k):
        return [send(10 + 8 * k, chip, k, side, {"tm": partner})]

    def start(copies):
        for one in copies:
            one.start()

    def row_piece(k):
        arrive(tm, k, col)
        start(spread(k))

    def edge_pieces(k):
        arrive(chip, k, col)
        start(pass_chip(k))
        arrive(tm, k, side)
        start(pass_side(k))

    def corner_piece(k):
        arrive(chip, k, side, 0)
        arrive(chip, k, side, 1)
        start(pass_corner(k))

    def from_core(k, q):
        arrive(partner, k, q)
        arrive(lax.rem(partner + 2, groups), k, q)

    mine = pltpu.make_async_copy(own_ref, held.at[tm, row * cols + col], own_sem)

    @pl.when(step == 0)
    def _():
        barrier = pltpu.get_barrier_semaphore()
        friends = [{"tm": chip}, {"col": side}, {"tm": partner}]
        friends += [{"row": row_at(k)} for k in (1, 2, 3)]
        for friend in friends:
            pl.semaphore_signal(barrier, inc=1, device_id=friend, device_id_type=mesh_id)
        pl.semaphore_wait(barrier, len(friends))
        first, second, third = own_sends()
        first.start()
        start(spread(0))
        second.start()
        mine.start()
        row_piece(1)
        third.start()
        edge_pieces(0)
        mine.wait()
        edge_pieces(1)
        from_core(0, col)
        from_core(1, col)

    @pl.when(step == 1)
    def _():
        row_piece(2)
        corner_piece(0)
        from_core(0, side)

    @pl.when(step == 3)
    def _():
        row_piece(3)
        edge_pieces(2)
        from_core(2, col)

    @pl.when(step == 5)
    def _():
        corner_piece(1)
        from_core(1, side)

    @pl.when(step == 7)
    def _():
        edge_pieces(3)
        from_core(3, col)

    @pl.when(step == 10)
    def _():
        corner_piece(2)
        from_core(2, side)

    @pl.when(step == 14)
    def _():
        corner_piece(3)
        from_core(3, side)

    now = jnp.minimum(step, count - 1)
    n, m = pair(now, core)
    a = block_at(n)
    b = block_at(m)
    before = jnp.maximum(step - 1, 0)

    def copies(at, kind, who):
        tn, tk = pair(at, who)
        first, second = (tn, tk) if kind == 0 else (tk, tn)
        where = lax.rem(at, 2)
        rows = pl.ds(pl.multiple_of(block_at(first) * BLOCK, BLOCK), BLOCK)
        columns = pl.ds(pl.multiple_of(block_at(second) * BLOCK, BLOCK), BLOCK)
        source = tile if kind == 0 else mirror
        kept = pltpu.make_async_copy(
            source.at[where, pl.ds(core * here, here)], out_ref.at[:, :, rows, columns],
            local_sem.at[kind, where],
        )
        given = pltpu.make_async_remote_copy(
            src_ref=source.at[where, pl.ds((1 - core) * here, here)],
            dst_ref=out_ref.at[:, :, rows, columns],
            send_sem=send_sem.at[kind, where],
            recv_sem=recv_sem.at[kind, at],
            device_id={"tm": partner},
            device_id_type=mesh_id,
        )
        return kept, given

    def begin(at, kind):
        kept, given = copies(at, kind, core)
        kept.start()
        given.start()

    def finish(at, kind):
        kept, given = copies(at, kind, core)
        kept.wait()
        given.wait_send()

    def turned(at, who):
        tn, tk = pair(at, who)
        return tn != tk

    @pl.when((step < count) & ((step == 0) | (n != pair(before, core)[0])))
    def _():
        @pl.loop(0, bins)
        def _(g):
            block = held[:, a, g]
            crossed = jnp.concatenate([-block[:, rec:], block[:, :rec]], axis=1)
            left[g, :BLOCK] = block.reshape(deep, BLOCK).T
            left[g, BLOCK:] = crossed.reshape(deep, BLOCK).T

    @pl.when(step >= 3)
    def _():
        @pl.when(turned(step - 3, core))
        def _():
            finish(step - 3, 1)

    def gram_of(g):
        both = jnp.dot(
            left[g], held[:, b, g].reshape(deep, BLOCK), preferred_element_type=jnp.float32
        ).astype(jnp.bfloat16)
        gram[0, g] = both[:BLOCK]
        gram[1, g] = both[BLOCK:]

    def turn(f):
        mirror[old, f, 0] = tile[old, f, 0].T
        mirror[old, f, 1] = -tile[old, f, 1].T

    per = bins // (2 * here)

    @pl.when(step < count)
    def _():
        @pl.loop(0, 2 * here)
        def _(f):
            for k in range(per):
                gram_of(f * per + k)
            turn(f)

    @pl.when(step == count)
    def _():
        @pl.loop(0, 2 * here)
        def _(f):
            turn(f)

    @pl.when(step >= 1)
    def _():
        @pl.when(turned(before, core))
        def _():
            begin(before, 1)

    @pl.when(step >= 2)
    def _():
        finish(step - 2, 0)

    @pl.when(step < count)
    def _():
        kernel = kmat_ref[0, shift[a * blocks + b]]

        @pl.loop(0, BLOCK // SUB // 4)
        def _(quad):
            for k in range(4):
                rows = pl.ds(pl.multiple_of((quad * 4 + k) * SUB, SUB), SUB)
                for c in range(2):
                    part = gram[c, :, rows, :].reshape(bins * SUB, BLOCK)
                    mixed = jnp.dot(kernel, part, preferred_element_type=jnp.float32)
                    tile[slot, :, c, rows, :] = mixed.astype(jnp.bfloat16).reshape(
                        2 * here, SUB, BLOCK
                    )

        begin(step, 0)

    @pl.when(step == count)
    def _():
        finish(count - 1, 0)
        for at in (count - 2, count - 1):
            @pl.when(turned(at, core))
            def _():
                finish(at, 1)

        @pl.loop(0, count)
        def _(at):
            copies(at, 0, 1 - core)[1].wait_recv()

            @pl.when(turned(at, 1 - core))
            def _():
                copies(at, 1, 1 - core)[1].wait_recv()

        for one in own_sends():
            one.wait_send()
        for k in range(bands):
            for one in spread(k) + pass_chip(k) + pass_side(k) + pass_corner(k):
                one.wait_send()


def fused_tiles(own, shift, kmats, groups, bands, cols, stations):
    bins, both, _ = own.shape
    here = bins // groups
    blocks = bands * cols
    count = blocks * (blocks + 1) // 4
    flops = count * bins * 2 * BLOCK * BLOCK * (groups * both * 2 + 4 * here * SUB)
    return pl.pallas_call(
        functools.partial(fused_kernel, groups, bands, cols, bins, both // 2, here),
        out_shape=jax.ShapeDtypeStruct((here, 2, stations, stations), jnp.bfloat16),
        grid_spec=pltpu.PrefetchScalarGridSpec(
            num_scalar_prefetch=1,
            grid=(count + 1,),
            in_specs=[
                pl.BlockSpec(memory_space=pl.ANY),
                pl.BlockSpec(
                    (1,) + kmats.shape[1:], lambda s, sh: (lax.axis_index("tm") // 2, 0, 0, 0)
                ),
            ],
            out_specs=pl.BlockSpec(memory_space=pl.ANY),
            scratch_shapes=[
                pltpu.VMEM((groups, blocks) + own.shape, jnp.bfloat16),
                pltpu.VMEM((bins, 2 * BLOCK, groups * both), jnp.bfloat16),
                pltpu.VMEM((2, bins, BLOCK, BLOCK), jnp.bfloat16),
                pltpu.VMEM((2, 2 * here, 2, BLOCK, BLOCK), jnp.bfloat16),
                pltpu.VMEM((2, 2 * here, 2, BLOCK, BLOCK), jnp.bfloat16),
                pltpu.SemaphoreType.DMA,
                pltpu.SemaphoreType.DMA((3 + 8 * bands,)),
                pltpu.SemaphoreType.DMA((2, groups, blocks)),
                pltpu.SemaphoreType.DMA((2, 2)),
                pltpu.SemaphoreType.DMA((2, 2)),
                pltpu.SemaphoreType.DMA((2, count)),
            ],
        ),
        compiler_params=pltpu.CompilerParams(
            vmem_limit_bytes=62 * 2**20, collective_id=1, has_side_effects=True
        ),
        cost_estimate=pl.CostEstimate(flops=flops, bytes_accessed=100 * 2**20, transcendentals=0),
        name="fused_tiles",
    )(shift, own, kmats)


def square_kernel(scale, place, rows_ref, cols_ref, out_ref):
    left_re = rows_ref[0, 0]
    left_im = rows_ref[0, 1]
    right_re = cols_ref[0, 0]
    right_im = cols_ref[0, 1]
    dot = functools.partial(jnp.dot, preferred_element_type=jnp.float32)
    squares = dot(left_re, right_re)
    crosses = dot(left_im, right_im)
    both = dot(left_re + left_im, right_re + right_im)
    out_ref[0, 0] = ((squares - crosses) * scale).astype(jnp.bfloat16)
    out_ref[1, 0] = ((both - squares - crosses) * scale).astype(jnp.bfloat16)


def square_tiles(windowed, place, tile_rows, tile_cols, scale):
    here, _, stations, _ = windowed.shape
    wide = min(512, tile_cols)
    count = tile_cols // wide
    return pl.pallas_call(
        functools.partial(square_kernel, scale),
        out_shape=jax.ShapeDtypeStruct((2, here, tile_rows, tile_cols), jnp.bfloat16),
        grid_spec=pltpu.PrefetchScalarGridSpec(
            num_scalar_prefetch=1,
            grid=(here, count),
            in_specs=[
                pl.BlockSpec((1, 2, tile_rows, stations), lambda f, j, p: (f, 0, p[0], 0)),
                pl.BlockSpec((1, 2, stations, wide), lambda f, j, p: (f, 0, 0, p[1] * count + j)),
            ],
            out_specs=pl.BlockSpec((2, 1, tile_rows, wide), lambda f, j, p: (0, f, 0, j)),
        ),
        compiler_params=pltpu.CompilerParams(vmem_limit_bytes=56 * 2**20),
        cost_estimate=pl.CostEstimate(
            flops=8 * here * tile_rows * tile_cols * stations,
            bytes_accessed=60 * 2**20,
            transcendentals=0,
        ),
        name="square_tiles",
    )(place, windowed, windowed)


def on_device(mesh, records, offsets):
    rec, _, bins, width = records.shape
    groups = mesh.shape["tm"]
    bands = mesh.shape["row"]
    stations = width * bands * mesh.shape["col"]
    here = bins // groups
    own = jnp.transpose(records, (2, 1, 0, 3)).reshape(bins, 2 * rec, width)
    cols = mesh.shape["col"]
    table = np.einsum("ofg,st->ofsgt", lag_table(bins), np.eye(SUB))
    table = table.reshape(NOFF, groups // 2, 2 * here * SUB, bins * SUB)
    kmats = jnp.asarray(np.moveaxis(table, 1, 0).astype(jnp.bfloat16))
    shift = ((offsets + offsets.T) % NOFF).reshape(-1)
    if width == BLOCK and (groups, bands, cols) == (4, 4, 2):
        windowed = fused_tiles(own, shift, kmats, groups, bands, cols, stations)
    else:
        band = lax.all_gather(own, "col", axis=2, tiled=True)
        spectra = lax.all_gather(band, ("tm", "row"), axis=0)
        spectra = spectra.reshape(groups, bands, bins, 2 * rec, stations // bands)
        kmat = lax.dynamic_index_in_dim(kmats, lax.axis_index("tm") // 2, 0, keepdims=False)
        windowed = windowed_tiles(spectra, shift, kmat, stations)
    place = jnp.stack([lax.axis_index("row"), lax.axis_index("col")]).astype(jnp.int32)
    scale = 1.0 / (rec * groups * math.sqrt(stations))
    return square_tiles(
        windowed, place, stations // bands, stations // mesh.shape["col"], scale
    )


def solution(mesh):
    return jax.shard_map(
        functools.partial(on_device, mesh),
        mesh=mesh,
        in_specs=(P("tm", None, None, ("row", "col")), P()),
        out_specs=P(None, "tm", "row", "col"),
        check_vma=False,
    )
```

```python
import functools
import math

import jax
import jax.numpy as jnp
import numpy as np
from jax import lax
from jax.experimental import pallas as pl
from jax.experimental.pallas import tpu as pltpu
from jax.sharding import PartitionSpec as P

BLOCK = 256
NOFF = 4
SUB = 16


def lag_table(bins):
    freq = np.arange(bins)
    lag = np.minimum(freq, bins - freq)
    starts = np.arange(NOFF)[:, None] + 2
    inside = (lag[None, :] >= starts) & (lag[None, :] < starts + 3)
    weights = np.where(inside, 1.0, 0.1)
    phase = (freq[:, None, None] - freq[None, :, None]) * freq[None, None, :] % bins
    cosines = np.cos(phase * (2.0 * math.pi / bins))
    return np.einsum("ot,fgt->ofg", weights, cosines) / bins


def pair_of(step, core, blocks):
    half = blocks // 2
    main = half * half
    tail = step // main
    row = (step // half) * (1 - tail) + (step - main) * tail
    return core * (half - half // 2 * tail) + row, (step % half) * (1 - tail) + half * tail


def tile_kernel(bins, groups, rec, here, blocks, shift, xa_ref, xb_ref, kmat_ref,
                out_ref, left, gram, tile, mirror, local_sem, send_sem, recv_sem):
    step = pl.program_id(0)
    count = pl.num_programs(0) - 1
    tm = lax.axis_index("tm")
    core = lax.rem(tm, 2)
    partner = tm + 1 - 2 * core
    half = blocks // 2
    deep = groups * 2 * rec
    slot = lax.rem(step, 2)
    a, d = pair_of(jnp.minimum(step, count - 1), core, blocks)
    b = lax.rem(a + d, blocks)

    def copies(at, kind):
        ta, td = pair_of(at, core, blocks)
        tb = lax.rem(ta + td, blocks)
        where = lax.rem(at, 2)
        first, second = (ta, tb) if kind == 0 else (tb, ta)
        rows = pl.ds(pl.multiple_of(first * BLOCK, BLOCK), BLOCK)
        cols = pl.ds(pl.multiple_of(second * BLOCK, BLOCK), BLOCK)
        held = tile if kind == 0 else mirror
        kept = pltpu.make_async_copy(
            held.at[where, pl.ds(core * here, here)], out_ref.at[:, :, rows, cols],
            local_sem.at[kind, where],
        )
        given = pltpu.make_async_remote_copy(
            src_ref=held.at[where, pl.ds((1 - core) * here, here)],
            dst_ref=out_ref.at[:, :, rows, cols],
            send_sem=send_sem.at[kind, where],
            recv_sem=recv_sem.at[kind, at],
            device_id={"tm": partner},
            device_id_type=pl.DeviceIdType.MESH,
        )
        return kept, given

    def begin(at, kind):
        kept, given = copies(at, kind)
        kept.start()
        given.start()

    def finish(at, kind):
        kept, given = copies(at, kind)
        kept.wait()
        given.wait_send()

    def turned(at):
        return pair_of(at, core, blocks)[1] > 0

    @pl.when(step == 0)
    def _():
        barrier = pltpu.get_barrier_semaphore()
        pl.semaphore_signal(
            barrier, inc=1, device_id={"tm": partner}, device_id_type=pl.DeviceIdType.MESH
        )
        pl.semaphore_wait(barrier, 1)

    @pl.when((step < count) & ((d == 0) | (step >= half * half)))
    def _():
        @pl.loop(0, bins)
        def _(g):
            block = xa_ref[:, 0, g]
            crossed = jnp.concatenate([-block[:, rec:], block[:, :rec]], axis=1)
            left[g, :BLOCK] = block.reshape(deep, BLOCK).T
            left[g, BLOCK:] = crossed.reshape(deep, BLOCK).T

    before = jnp.maximum(step - 1, 0)
    old = lax.rem(step + 1, 2)

    @pl.when(step >= 3)
    def _():
        @pl.when(turned(step - 3))
        def _():
            finish(step - 3, 1)

    def gram_of(g):
        both = jnp.dot(
            left[g], xb_ref[:, 0, g].reshape(deep, BLOCK), preferred_element_type=jnp.float32
        ).astype(jnp.bfloat16)
        gram[0, g] = both[:BLOCK]
        gram[1, g] = both[BLOCK:]

    def turn(f):
        mirror[old, f, 0] = tile[old, f, 0].T
        mirror[old, f, 1] = -tile[old, f, 1].T

    per = bins // (2 * here)

    @pl.when(step < count)
    def _():
        @pl.loop(0, 2 * here)
        def _(f):
            for k in range(per):
                gram_of(f * per + k)
            turn(f)

    @pl.when(step == count)
    def _():
        @pl.loop(0, 2 * here)
        def _(f):
            turn(f)

    @pl.when(step >= 1)
    def _():
        @pl.when(turned(before))
        def _():
            begin(before, 1)

    @pl.when(step >= 2)
    def _():
        finish(step - 2, 0)

    @pl.when(step < count)
    def _():
        kernel = kmat_ref[shift[a * blocks + b]]

        @pl.loop(0, BLOCK // SUB // 4)
        def _(quad):
            for k in range(4):
                rows = pl.ds(pl.multiple_of((quad * 4 + k) * SUB, SUB), SUB)
                for c in range(2):
                    part = gram[c, :, rows, :].reshape(bins * SUB, BLOCK)
                    mixed = jnp.dot(kernel, part, preferred_element_type=jnp.float32)
                    tile[slot, :, c, rows, :] = mixed.astype(jnp.bfloat16).reshape(
                        2 * here, SUB, BLOCK
                    )

        begin(step, 0)

    @pl.when(step == count)
    def _():
        finish(count - 1, 0)
        for at in (count - 2, count - 1):
            @pl.when(turned(at))
            def _():
                finish(at, 1)

        @pl.loop(0, count)
        def _(at):
            copies(at, 0)[1].wait_recv()

            @pl.when(turned(at))
            def _():
                copies(at, 1)[1].wait_recv()


def windowed_tiles(spectra, shift, kmat, stations):
    groups, bands, bins, both, width = spectra.shape
    rec = both // 2
    here = bins // groups
    per = width // BLOCK
    blocks = stations // BLOCK
    count = blocks * (blocks + 1) // 4
    block = (groups, 1, bins, both, BLOCK)
    flops = count * bins * 2 * BLOCK * BLOCK * (groups * both * 2 + 4 * here * SUB)

    def pick_a(s, sh):
        a, _ = pair_of(jnp.minimum(s, count - 1), lax.rem(lax.axis_index("tm"), 2), blocks)
        return (0, a // per, 0, 0, lax.rem(a, per))

    def pick_b(s, sh):
        a, d = pair_of(jnp.minimum(s, count - 1), lax.rem(lax.axis_index("tm"), 2), blocks)
        b = lax.rem(a + d, blocks)
        return (0, b // per, 0, 0, lax.rem(b, per))

    return pl.pallas_call(
        functools.partial(tile_kernel, bins, groups, rec, here, blocks),
        out_shape=jax.ShapeDtypeStruct((here, 2, stations, stations), jnp.bfloat16),
        grid_spec=pltpu.PrefetchScalarGridSpec(
            num_scalar_prefetch=1,
            grid=(count + 1,),
            in_specs=[
                pl.BlockSpec(block, pick_a),
                pl.BlockSpec(block, pick_b),
                pl.BlockSpec(kmat.shape, lambda s, sh: (0, 0, 0)),
            ],
            out_specs=pl.BlockSpec(memory_space=pl.ANY),
            scratch_shapes=[
                pltpu.VMEM((bins, 2 * BLOCK, groups * both), jnp.bfloat16),
                pltpu.VMEM((2, bins, BLOCK, BLOCK), jnp.bfloat16),
                pltpu.VMEM((2, 2 * here, 2, BLOCK, BLOCK), jnp.bfloat16),
                pltpu.VMEM((2, 2 * here, 2, BLOCK, BLOCK), jnp.bfloat16),
                pltpu.SemaphoreType.DMA((2, 2)),
                pltpu.SemaphoreType.DMA((2, 2)),
                pltpu.SemaphoreType.DMA((2, count)),
            ],
        ),
        compiler_params=pltpu.CompilerParams(
            vmem_limit_bytes=60 * 2**20, collective_id=0, has_side_effects=True
        ),
        cost_estimate=pl.CostEstimate(flops=flops, bytes_accessed=200 * 2**20, transcendentals=0),
        name="windowed_tiles",
    )(shift, spectra, spectra, kmat)


def fused_kernel(groups, bands, cols, bins, rec, here, shift, own_ref, kmat_ref, out_ref,
                 held, left, gram, tile, mirror, own_sem, piece_send, piece_recv,
                 local_sem, send_sem, recv_sem):
    step = pl.program_id(0)
    count = pl.num_programs(0) - 1
    tm = lax.axis_index("tm")
    row = lax.axis_index("row")
    col = lax.axis_index("col")
    core = lax.rem(tm, 2)
    partner = tm + 1 - 2 * core
    blocks = bands * cols
    deep = groups * 2 * rec
    slot = lax.rem(step, 2)
    old = lax.rem(step + 1, 2)
    mesh_id = pl.DeviceIdType.MESH
    chip = lax.rem(tm + 2, groups)
    side = lax.rem(col + 1, cols)
    bin_half = bins // 2
    middle = (row == 1) | (row == 2)
    arrival = [(0, 0), (1, 0), (0, 1), (2, 0), (1, 1), (3, 0), (2, 1), (3, 1)]

    def row_at(k):
        high = row // 2
        return (row, row + 1 - 2 * lax.rem(row, 2), 2 - high, 3 - 3 * high)[k]

    def block_at(n):
        total = 0
        for index, (k, other) in enumerate(arrival):
            where = row_at(k) * cols + (side if other else col)
            total = total + jnp.where(n == index, where, 0)
        return total

    def pair(at, who):
        t = 2 * at + who
        n = 0
        for index in range(1, blocks):
            n = n + jnp.minimum(t // (index * (index + 1) // 2), 1)
        return n, t - n * (n + 1) // 2

    def send(index, t, k, q, target, part=None, source=None):
        block = row_at(k) * cols + q
        there = held.at[t, block]
        source = there if source is None else source
        if part is not None:
            source = source.at[pl.ds(part * bin_half, bin_half)]
            there = there.at[pl.ds(part * bin_half, bin_half)]
        return pltpu.make_async_remote_copy(
            src_ref=source, dst_ref=there, send_sem=piece_send.at[index],
            recv_sem=piece_recv.at[part or 0, t, block], device_id=target, device_id_type=mesh_id,
        )

    def arrive(t, k, q, part=None):
        block = row_at(k) * cols + q
        piece = held.at[t, block]
        if part is not None:
            piece = piece.at[pl.ds(part * bin_half, bin_half)]
        pltpu.make_async_copy(piece, piece, piece_recv.at[part or 0, t, block]).wait()

    def own_sends():
        return [send(0, tm, 0, col, {"row": row_at(1)}, source=own_ref)]

    def relays():
        over, back = {"row": row_at(2)}, {"row": row_at(1)}
        return [
            send(1, tm, 0, col, over, source=own_ref),
            send(2, tm, 1, col, over),
            send(3, tm, 2, col, back),
            send(4, tm, 3, col, back),
        ]

    def spread(k):
        source = own_ref if k == 0 else None
        base = 5 + 8 * k
        return [
            send(base, tm, k, col, {"tm": chip}, source=source),
            send(base + 1, tm, k, col, {"col": side}, source=source),
            send(base + 2, tm, k, col, {"tm": partner}, source=source),
        ]

    def pass_chip(k):
        base = 8 + 8 * k
        return [
            send(base, chip, k, col, {"col": side}, 0),
            send(base + 1, chip, k, col, {"tm": partner}),
        ]

    def pass_side(k):
        base = 10 + 8 * k
        return [
            send(base, tm, k, side, {"tm": chip}, 1),
            send(base + 1, tm, k, side, {"tm": partner}),
        ]

    def pass_corner(k):
        return [send(12 + 8 * k, chip, k, side, {"tm": partner})]

    def start(copies):
        for one in copies:
            one.start()

    def relay(k):
        @pl.when(middle)
        def _():
            relays()[k].start()

    def row_piece(k):
        arrive(tm, k, col)
        relay(k)
        start(spread(k))

    def edge_pieces(k):
        arrive(chip, k, col)
        start(pass_chip(k))
        arrive(tm, k, side)
        start(pass_side(k))

    def corner_piece(k):
        arrive(chip, k, side, 0)
        arrive(chip, k, side, 1)
        start(pass_corner(k))

    def from_core(k, q):
        arrive(partner, k, q)
        arrive(lax.rem(partner + 2, groups), k, q)

    mine = pltpu.make_async_copy(own_ref, held.at[tm, row * cols + col], own_sem)

    @pl.when(step == 0)
    def _():
        barrier = pltpu.get_barrier_semaphore()
        friends = [{"tm": chip}, {"col": side}, {"tm": partner}]
        friends += [{"row": row_at(k)} for k in (1, 2, 3)]
        for friend in friends:
            pl.semaphore_signal(barrier, inc=1, device_id=friend, device_id_type=mesh_id)
        pl.semaphore_wait(barrier, len(friends))
        start(own_sends())
        relay(0)
        start(spread(0))
        mine.start()
        row_piece(1)
        edge_pieces(0)
        row_piece(2)
        mine.wait()
        edge_pieces(1)
        from_core(0, col)
        from_core(1, col)

    @pl.when(step == 1)
    def _():
        corner_piece(0)
        row_piece(3)
        from_core(0, side)

    @pl.when(step == 3)
    def _():
        edge_pieces(2)
        from_core(2, col)

    @pl.when(step == 5)
    def _():
        corner_piece(1)
        from_core(1, side)

    @pl.when(step == 7)
    def _():
        edge_pieces(3)
        from_core(3, col)

    @pl.when(step == 10)
    def _():
        corner_piece(2)
        from_core(2, side)

    @pl.when(step == 14)
    def _():
        corner_piece(3)
        from_core(3, side)

    now = jnp.minimum(step, count - 1)
    n, m = pair(now, core)
    a = block_at(n)
    b = block_at(m)
    before = jnp.maximum(step - 1, 0)

    def copies(at, kind, who):
        tn, tk = pair(at, who)
        first, second = (tn, tk) if kind == 0 else (tk, tn)
        where = lax.rem(at, 2)
        rows = pl.ds(pl.multiple_of(block_at(first) * BLOCK, BLOCK), BLOCK)
        columns = pl.ds(pl.multiple_of(block_at(second) * BLOCK, BLOCK), BLOCK)
        source = tile if kind == 0 else mirror
        kept = pltpu.make_async_copy(
            source.at[where, pl.ds(core * here, here)], out_ref.at[:, :, rows, columns],
            local_sem.at[kind, where],
        )
        given = pltpu.make_async_remote_copy(
            src_ref=source.at[where, pl.ds((1 - core) * here, here)],
            dst_ref=out_ref.at[:, :, rows, columns],
            send_sem=send_sem.at[kind, where],
            recv_sem=recv_sem.at[kind, at],
            device_id={"tm": partner},
            device_id_type=mesh_id,
        )
        return kept, given

    def begin(at, kind):
        kept, given = copies(at, kind, core)
        kept.start()
        given.start()

    def finish(at, kind):
        kept, given = copies(at, kind, core)
        kept.wait()
        given.wait_send()

    def turned(at, who):
        tn, tk = pair(at, who)
        return tn != tk

    @pl.when(step >= 3)
    def _():
        @pl.when(turned(step - 3, core))
        def _():
            finish(step - 3, 1)

    def load(g):
        left[g] = held[:, a, g].reshape(deep, BLOCK).T

    def gram_of(g):
        block = held[:, b, g]
        crossed = jnp.concatenate([block[:, rec:], -block[:, :rec]], axis=1)
        right = jnp.concatenate(
            [block.reshape(deep, BLOCK), crossed.reshape(deep, BLOCK)], axis=1
        )
        both = jnp.dot(left[g], right, preferred_element_type=jnp.float32).astype(jnp.bfloat16)
        gram[0, g] = both[:, :BLOCK]
        gram[1, g] = both[:, BLOCK:]

    def turn(f):
        mirror[old, f, 0] = tile[old, f, 0].T
        mirror[old, f, 1] = -tile[old, f, 1].T

    per = bins // (2 * here)

    fresh = (step == 0) | (n != pair(before, core)[0])

    @pl.when((step < count) & fresh)
    def _():
        for k in range(per):
            load(k)

        @pl.loop(0, 2 * here)
        def _(f):
            for k in range(per):
                gram_of(f * per + k)
            turn(f)
            for k in range(per):
                load(lax.rem(f + 1, 2 * here) * per + k)

    @pl.when((step < count) & jnp.logical_not(fresh))
    def _():
        @pl.loop(0, 2 * here)
        def _(f):
            for k in range(per):
                gram_of(f * per + k)
            turn(f)

    @pl.when(step == count)
    def _():
        @pl.loop(0, 2 * here)
        def _(f):
            turn(f)

    @pl.when(step >= 1)
    def _():
        @pl.when(turned(before, core))
        def _():
            begin(before, 1)

    @pl.when(step >= 2)
    def _():
        finish(step - 2, 0)

    @pl.when(step < count)
    def _():
        kernel = kmat_ref[0, shift[a * blocks + b]]

        @pl.loop(0, BLOCK // SUB // 4)
        def _(quad):
            for k in range(4):
                rows = pl.ds(pl.multiple_of((quad * 4 + k) * SUB, SUB), SUB)
                for c in range(2):
                    part = gram[c, :, rows, :].reshape(bins * SUB, BLOCK)
                    mixed = jnp.dot(kernel, part, preferred_element_type=jnp.float32)
                    tile[slot, :, c, rows, :] = mixed.astype(jnp.bfloat16).reshape(
                        2 * here, SUB, BLOCK
                    )

        begin(step, 0)

    @pl.when(step == count)
    def _():
        finish(count - 1, 0)
        for at in (count - 2, count - 1):
            @pl.when(turned(at, core))
            def _():
                finish(at, 1)

        @pl.loop(0, count)
        def _(at):
            copies(at, 0, 1 - core)[1].wait_recv()

            @pl.when(turned(at, 1 - core))
            def _():
                copies(at, 1, 1 - core)[1].wait_recv()

        for one in own_sends():
            one.wait_send()

        @pl.when(middle)
        def _():
            for one in relays():
                one.wait_send()

        for k in range(bands):
            for one in spread(k) + pass_chip(k) + pass_side(k) + pass_corner(k):
                one.wait_send()


def fused_tiles(own, shift, kmats, groups, bands, cols, stations):
    bins, both, _ = own.shape
    here = bins // groups
    blocks = bands * cols
    count = blocks * (blocks + 1) // 4
    flops = count * bins * 2 * BLOCK * BLOCK * (groups * both * 2 + 4 * here * SUB)
    return pl.pallas_call(
        functools.partial(fused_kernel, groups, bands, cols, bins, both // 2, here),
        out_shape=jax.ShapeDtypeStruct((here, 2, stations, stations), jnp.bfloat16),
        grid_spec=pltpu.PrefetchScalarGridSpec(
            num_scalar_prefetch=1,
            grid=(count + 1,),
            in_specs=[
                pl.BlockSpec(memory_space=pl.ANY),
                pl.BlockSpec(
                    (1,) + kmats.shape[1:], lambda s, sh: (lax.axis_index("tm") // 2, 0, 0, 0)
                ),
            ],
            out_specs=pl.BlockSpec(memory_space=pl.ANY),
            scratch_shapes=[
                pltpu.VMEM((groups, blocks) + own.shape, jnp.bfloat16),
                pltpu.VMEM((bins, BLOCK, groups * both), jnp.bfloat16),
                pltpu.VMEM((2, bins, BLOCK, BLOCK), jnp.bfloat16),
                pltpu.VMEM((2, 2 * here, 2, BLOCK, BLOCK), jnp.bfloat16),
                pltpu.VMEM((2, 2 * here, 2, BLOCK, BLOCK), jnp.bfloat16),
                pltpu.SemaphoreType.DMA,
                pltpu.SemaphoreType.DMA((5 + 8 * bands,)),
                pltpu.SemaphoreType.DMA((2, groups, blocks)),
                pltpu.SemaphoreType.DMA((2, 2)),
                pltpu.SemaphoreType.DMA((2, 2)),
                pltpu.SemaphoreType.DMA((2, count)),
            ],
        ),
        compiler_params=pltpu.CompilerParams(
            vmem_limit_bytes=62 * 2**20, collective_id=1, has_side_effects=True
        ),
        cost_estimate=pl.CostEstimate(flops=flops, bytes_accessed=100 * 2**20, transcendentals=0),
        name="fused_tiles",
    )(shift, own, kmats)


def square_kernel(scale, place, rows_ref, cols_ref, out_ref):
    left_re = rows_ref[0, 0]
    left_im = rows_ref[0, 1]
    right_re = cols_ref[0, 0]
    right_im = cols_ref[0, 1]
    dot = functools.partial(jnp.dot, preferred_element_type=jnp.float32)
    squares = dot(left_re, right_re)
    crosses = dot(left_im, right_im)
    both = dot(left_re + left_im, right_re + right_im)
    out_ref[0, 0] = ((squares - crosses) * scale).astype(jnp.bfloat16)
    out_ref[1, 0] = ((both - squares - crosses) * scale).astype(jnp.bfloat16)


def square_tiles(windowed, place, tile_rows, tile_cols, scale):
    here, _, stations, _ = windowed.shape
    wide = min(512, tile_cols)
    count = tile_cols // wide
    return pl.pallas_call(
        functools.partial(square_kernel, scale),
        out_shape=jax.ShapeDtypeStruct((2, here, tile_rows, tile_cols), jnp.bfloat16),
        grid_spec=pltpu.PrefetchScalarGridSpec(
            num_scalar_prefetch=1,
            grid=(here, count),
            in_specs=[
                pl.BlockSpec((1, 2, tile_rows, stations), lambda f, j, p: (f, 0, p[0], 0)),
                pl.BlockSpec((1, 2, stations, wide), lambda f, j, p: (f, 0, 0, p[1] * count + j)),
            ],
            out_specs=pl.BlockSpec((2, 1, tile_rows, wide), lambda f, j, p: (0, f, 0, j)),
        ),
        compiler_params=pltpu.CompilerParams(vmem_limit_bytes=56 * 2**20),
        cost_estimate=pl.CostEstimate(
            flops=8 * here * tile_rows * tile_cols * stations,
            bytes_accessed=60 * 2**20,
            transcendentals=0,
        ),
        name="square_tiles",
    )(place, windowed, windowed)


def on_device(mesh, records, offsets):
    rec, _, bins, width = records.shape
    groups = mesh.shape["tm"]
    bands = mesh.shape["row"]
    stations = width * bands * mesh.shape["col"]
    here = bins // groups
    own = jnp.transpose(records, (2, 1, 0, 3)).reshape(bins, 2 * rec, width)
    cols = mesh.shape["col"]
    table = np.einsum("ofg,st->ofsgt", lag_table(bins), np.eye(SUB))
    table = table.reshape(NOFF, groups // 2, 2 * here * SUB, bins * SUB)
    kmats = jnp.asarray(np.moveaxis(table, 1, 0).astype(jnp.bfloat16))
    shift = ((offsets + offsets.T) % NOFF).reshape(-1)
    if width == BLOCK and (groups, bands, cols) == (4, 4, 2):
        windowed = fused_tiles(own, shift, kmats, groups, bands, cols, stations)
    else:
        band = lax.all_gather(own, "col", axis=2, tiled=True)
        spectra = lax.all_gather(band, ("tm", "row"), axis=0)
        spectra = spectra.reshape(groups, bands, bins, 2 * rec, stations // bands)
        kmat = lax.dynamic_index_in_dim(kmats, lax.axis_index("tm") // 2, 0, keepdims=False)
        windowed = windowed_tiles(spectra, shift, kmat, stations)
    place = jnp.stack([lax.axis_index("row"), lax.axis_index("col")]).astype(jnp.int32)
    scale = 1.0 / (rec * groups * math.sqrt(stations))
    return square_tiles(
        windowed, place, stations // bands, stations // mesh.shape["col"], scale
    )


def solution(mesh):
    return jax.shard_map(
        functools.partial(on_device, mesh),
        mesh=mesh,
        in_specs=(P("tm", None, None, ("row", "col")), P()),
        out_specs=P(None, "tm", "row", "col"),
        check_vma=False,
    )
```

```python
import functools
import math

import jax
import jax.numpy as jnp
import numpy as np
from jax import lax
from jax.experimental import pallas as pl
from jax.experimental.pallas import tpu as pltpu
from jax.sharding import PartitionSpec as P

BLOCK = 256
NOFF = 4
SUB = 16


def lag_table(bins):
    freq = np.arange(bins)
    lag = np.minimum(freq, bins - freq)
    starts = np.arange(NOFF)[:, None] + 2
    inside = (lag[None, :] >= starts) & (lag[None, :] < starts + 3)
    weights = np.where(inside, 1.0, 0.1)
    phase = (freq[:, None, None] - freq[None, :, None]) * freq[None, None, :] % bins
    cosines = np.cos(phase * (2.0 * math.pi / bins))
    return np.einsum("ot,fgt->ofg", weights, cosines) / bins


def pair_of(step, core, blocks):
    half = blocks // 2
    main = half * half
    tail = step // main
    row = (step // half) * (1 - tail) + (step - main) * tail
    return core * (half - half // 2 * tail) + row, (step % half) * (1 - tail) + half * tail


def tile_kernel(bins, groups, rec, here, blocks, shift, xa_ref, xb_ref, kmat_ref,
                out_ref, left, gram, tile, mirror, local_sem, send_sem, recv_sem):
    step = pl.program_id(0)
    count = pl.num_programs(0) - 1
    tm = lax.axis_index("tm")
    core = lax.rem(tm, 2)
    partner = tm + 1 - 2 * core
    half = blocks // 2
    deep = groups * 2 * rec
    slot = lax.rem(step, 2)
    a, d = pair_of(jnp.minimum(step, count - 1), core, blocks)
    b = lax.rem(a + d, blocks)

    def copies(at, kind):
        ta, td = pair_of(at, core, blocks)
        tb = lax.rem(ta + td, blocks)
        where = lax.rem(at, 2)
        first, second = (ta, tb) if kind == 0 else (tb, ta)
        rows = pl.ds(pl.multiple_of(first * BLOCK, BLOCK), BLOCK)
        cols = pl.ds(pl.multiple_of(second * BLOCK, BLOCK), BLOCK)
        held = tile if kind == 0 else mirror
        kept = pltpu.make_async_copy(
            held.at[where, pl.ds(core * here, here)], out_ref.at[:, :, rows, cols],
            local_sem.at[kind, where],
        )
        given = pltpu.make_async_remote_copy(
            src_ref=held.at[where, pl.ds((1 - core) * here, here)],
            dst_ref=out_ref.at[:, :, rows, cols],
            send_sem=send_sem.at[kind, where],
            recv_sem=recv_sem.at[kind, at],
            device_id={"tm": partner},
            device_id_type=pl.DeviceIdType.MESH,
        )
        return kept, given

    def begin(at, kind):
        kept, given = copies(at, kind)
        kept.start()
        given.start()

    def finish(at, kind):
        kept, given = copies(at, kind)
        kept.wait()
        given.wait_send()

    def turned(at):
        return pair_of(at, core, blocks)[1] > 0

    @pl.when(step == 0)
    def _():
        barrier = pltpu.get_barrier_semaphore()
        pl.semaphore_signal(
            barrier, inc=1, device_id={"tm": partner}, device_id_type=pl.DeviceIdType.MESH
        )
        pl.semaphore_wait(barrier, 1)

    @pl.when((step < count) & ((d == 0) | (step >= half * half)))
    def _():
        @pl.loop(0, bins)
        def _(g):
            block = xa_ref[:, 0, g]
            crossed = jnp.concatenate([-block[:, rec:], block[:, :rec]], axis=1)
            left[g, :BLOCK] = block.reshape(deep, BLOCK).T
            left[g, BLOCK:] = crossed.reshape(deep, BLOCK).T

    before = jnp.maximum(step - 1, 0)
    old = lax.rem(step + 1, 2)

    @pl.when(step >= 3)
    def _():
        @pl.when(turned(step - 3))
        def _():
            finish(step - 3, 1)

    def gram_of(g):
        both = jnp.dot(
            left[g], xb_ref[:, 0, g].reshape(deep, BLOCK), preferred_element_type=jnp.float32
        ).astype(jnp.bfloat16)
        gram[0, g] = both[:BLOCK]
        gram[1, g] = both[BLOCK:]

    def turn(f):
        mirror[old, f, 0] = tile[old, f, 0].T
        mirror[old, f, 1] = -tile[old, f, 1].T

    per = bins // (2 * here)

    @pl.when(step < count)
    def _():
        @pl.loop(0, 2 * here)
        def _(f):
            for k in range(per):
                gram_of(f * per + k)
            turn(f)

    @pl.when(step == count)
    def _():
        @pl.loop(0, 2 * here)
        def _(f):
            turn(f)

    @pl.when(step >= 1)
    def _():
        @pl.when(turned(before))
        def _():
            begin(before, 1)

    @pl.when(step >= 2)
    def _():
        finish(step - 2, 0)

    @pl.when(step < count)
    def _():
        kernel = kmat_ref[shift[a * blocks + b]]

        @pl.loop(0, BLOCK // SUB // 4)
        def _(quad):
            for k in range(4):
                rows = pl.ds(pl.multiple_of((quad * 4 + k) * SUB, SUB), SUB)
                for c in range(2):
                    part = gram[c, :, rows, :].reshape(bins * SUB, BLOCK)
                    mixed = jnp.dot(kernel, part, preferred_element_type=jnp.float32)
                    tile[slot, :, c, rows, :] = mixed.astype(jnp.bfloat16).reshape(
                        2 * here, SUB, BLOCK
                    )

        begin(step, 0)

    @pl.when(step == count)
    def _():
        finish(count - 1, 0)
        for at in (count - 2, count - 1):
            @pl.when(turned(at))
            def _():
                finish(at, 1)

        @pl.loop(0, count)
        def _(at):
            copies(at, 0)[1].wait_recv()

            @pl.when(turned(at))
            def _():
                copies(at, 1)[1].wait_recv()


def windowed_tiles(spectra, shift, kmat, stations):
    groups, bands, bins, both, width = spectra.shape
    rec = both // 2
    here = bins // groups
    per = width // BLOCK
    blocks = stations // BLOCK
    count = blocks * (blocks + 1) // 4
    block = (groups, 1, bins, both, BLOCK)
    flops = count * bins * 2 * BLOCK * BLOCK * (groups * both * 2 + 4 * here * SUB)

    def pick_a(s, sh):
        a, _ = pair_of(jnp.minimum(s, count - 1), lax.rem(lax.axis_index("tm"), 2), blocks)
        return (0, a // per, 0, 0, lax.rem(a, per))

    def pick_b(s, sh):
        a, d = pair_of(jnp.minimum(s, count - 1), lax.rem(lax.axis_index("tm"), 2), blocks)
        b = lax.rem(a + d, blocks)
        return (0, b // per, 0, 0, lax.rem(b, per))

    return pl.pallas_call(
        functools.partial(tile_kernel, bins, groups, rec, here, blocks),
        out_shape=jax.ShapeDtypeStruct((here, 2, stations, stations), jnp.bfloat16),
        grid_spec=pltpu.PrefetchScalarGridSpec(
            num_scalar_prefetch=1,
            grid=(count + 1,),
            in_specs=[
                pl.BlockSpec(block, pick_a),
                pl.BlockSpec(block, pick_b),
                pl.BlockSpec(kmat.shape, lambda s, sh: (0, 0, 0)),
            ],
            out_specs=pl.BlockSpec(memory_space=pl.ANY),
            scratch_shapes=[
                pltpu.VMEM((bins, 2 * BLOCK, groups * both), jnp.bfloat16),
                pltpu.VMEM((2, bins, BLOCK, BLOCK), jnp.bfloat16),
                pltpu.VMEM((2, 2 * here, 2, BLOCK, BLOCK), jnp.bfloat16),
                pltpu.VMEM((2, 2 * here, 2, BLOCK, BLOCK), jnp.bfloat16),
                pltpu.SemaphoreType.DMA((2, 2)),
                pltpu.SemaphoreType.DMA((2, 2)),
                pltpu.SemaphoreType.DMA((2, count)),
            ],
        ),
        compiler_params=pltpu.CompilerParams(
            vmem_limit_bytes=60 * 2**20, collective_id=0, has_side_effects=True
        ),
        cost_estimate=pl.CostEstimate(flops=flops, bytes_accessed=200 * 2**20, transcendentals=0),
        name="windowed_tiles",
    )(shift, spectra, spectra, kmat)


def fused_kernel(groups, bands, cols, bins, rec, here, shift, own_ref, kmat_ref, out_ref,
                 held, left, gram, tile, mirror, own_sem, piece_send, piece_recv,
                 local_sem, send_sem, recv_sem):
    step = pl.program_id(0)
    count = pl.num_programs(0) - 1
    tm = lax.axis_index("tm")
    row = lax.axis_index("row")
    col = lax.axis_index("col")
    core = lax.rem(tm, 2)
    partner = tm + 1 - 2 * core
    blocks = bands * cols
    deep = groups * 2 * rec
    slot = lax.rem(step, 2)
    old = lax.rem(step + 1, 2)
    mesh_id = pl.DeviceIdType.MESH
    chip = lax.rem(tm + 2, groups)
    side = lax.rem(col + 1, cols)
    bin_half = bins // 2
    middle = (row == 1) | (row == 2)
    arrival = [(0, 0), (1, 0), (0, 1), (2, 0), (1, 1), (3, 0), (2, 1), (3, 1)]

    def row_at(k):
        high = row // 2
        return (row, row + 1 - 2 * lax.rem(row, 2), 2 - high, 3 - 3 * high)[k]

    def block_at(n):
        total = 0
        for index, (k, other) in enumerate(arrival):
            where = row_at(k) * cols + (side if other else col)
            total = total + jnp.where(n == index, where, 0)
        return total

    def pair(at, who):
        t = 2 * at + who
        n = 0
        for index in range(1, blocks):
            n = n + jnp.minimum(t // (index * (index + 1) // 2), 1)
        return n, t - n * (n + 1) // 2

    def send(index, t, k, q, target, part=None, source=None):
        block = row_at(k) * cols + q
        there = held.at[t, block]
        source = there if source is None else source
        if part is not None:
            source = source.at[pl.ds(part * bin_half, bin_half)]
            there = there.at[pl.ds(part * bin_half, bin_half)]
        return pltpu.make_async_remote_copy(
            src_ref=source, dst_ref=there, send_sem=piece_send.at[index],
            recv_sem=piece_recv.at[part or 0, t, block], device_id=target, device_id_type=mesh_id,
        )

    def arrive(t, k, q, part=None):
        block = row_at(k) * cols + q
        piece = held.at[t, block]
        if part is not None:
            piece = piece.at[pl.ds(part * bin_half, bin_half)]
        pltpu.make_async_copy(piece, piece, piece_recv.at[part or 0, t, block]).wait()

    def own_sends():
        return [send(0, tm, 0, col, {"row": row_at(1)}, source=own_ref)]

    def relays():
        over, back = {"row": row_at(2)}, {"row": row_at(1)}
        return [
            send(1, tm, 0, col, over, source=own_ref),
            send(2, tm, 1, col, over),
            send(3, tm, 2, col, back),
            send(4, tm, 3, col, back),
        ]

    def spread(k):
        source = own_ref if k == 0 else None
        base = 5 + 8 * k
        return [
            send(base, tm, k, col, {"tm": chip}, source=source),
            send(base + 1, tm, k, col, {"col": side}, source=source),
            send(base + 2, tm, k, col, {"tm": partner}, source=source),
        ]

    def pass_chip(k):
        base = 8 + 8 * k
        return [
            send(base, chip, k, col, {"col": side}, 0),
            send(base + 1, chip, k, col, {"tm": partner}),
        ]

    def pass_side(k):
        base = 10 + 8 * k
        return [
            send(base, tm, k, side, {"tm": chip}, 1),
            send(base + 1, tm, k, side, {"tm": partner}),
        ]

    def pass_corner(k):
        return [send(12 + 8 * k, chip, k, side, {"tm": partner})]

    def start(copies):
        for one in copies:
            one.start()

    def relay(k):
        @pl.when(middle)
        def _():
            relays()[k].start()

    def row_piece(k):
        arrive(tm, k, col)
        relay(k)
        start(spread(k))

    def edge_pieces(k):
        arrive(chip, k, col)
        start(pass_chip(k))
        arrive(tm, k, side)
        start(pass_side(k))

    def corner_piece(k):
        arrive(chip, k, side, 0)
        arrive(chip, k, side, 1)
        start(pass_corner(k))

    def from_core(k, q):
        arrive(partner, k, q)
        arrive(lax.rem(partner + 2, groups), k, q)

    mine = pltpu.make_async_copy(own_ref, held.at[tm, row * cols + col], own_sem)

    @pl.when(step == 0)
    def _():
        barrier = pltpu.get_barrier_semaphore()
        friends = [{"tm": chip}, {"col": side}, {"tm": partner}]
        friends += [{"row": row_at(k)} for k in (1, 2, 3)]
        for friend in friends:
            pl.semaphore_signal(barrier, inc=1, device_id=friend, device_id_type=mesh_id)
        pl.semaphore_wait(barrier, len(friends))
        start(own_sends())
        relay(0)
        start(spread(0))
        mine.start()
        row_piece(1)
        edge_pieces(0)
        row_piece(2)
        mine.wait()
        edge_pieces(1)
        from_core(0, col)
        from_core(1, col)

    @pl.when(step == 1)
    def _():
        corner_piece(0)
        row_piece(3)
        from_core(0, side)

    @pl.when(step == 3)
    def _():
        edge_pieces(2)
        from_core(2, col)

    @pl.when(step == 5)
    def _():
        corner_piece(1)
        from_core(1, side)

    @pl.when(step == 7)
    def _():
        edge_pieces(3)
        from_core(3, col)

    @pl.when(step == 10)
    def _():
        corner_piece(2)
        from_core(2, side)

    @pl.when(step == 14)
    def _():
        corner_piece(3)
        from_core(3, side)

    now = jnp.minimum(step, count - 1)
    n, m = pair(now, core)
    a = block_at(n)
    b = block_at(m)
    before = jnp.maximum(step - 1, 0)

    def copies(at, kind, who):
        tn, tk = pair(at, who)
        first, second = (tn, tk) if kind == 0 else (tk, tn)
        where = lax.rem(at, 2)
        rows = pl.ds(pl.multiple_of(block_at(first) * BLOCK, BLOCK), BLOCK)
        columns = pl.ds(pl.multiple_of(block_at(second) * BLOCK, BLOCK), BLOCK)
        source = tile if kind == 0 else mirror
        kept = pltpu.make_async_copy(
            source.at[where, pl.ds(core * here, here)], out_ref.at[:, :, rows, columns],
            local_sem.at[kind, where],
        )
        given = pltpu.make_async_remote_copy(
            src_ref=source.at[where, pl.ds((1 - core) * here, here)],
            dst_ref=out_ref.at[:, :, rows, columns],
            send_sem=send_sem.at[kind, where],
            recv_sem=recv_sem.at[kind, at],
            device_id={"tm": partner},
            device_id_type=mesh_id,
        )
        return kept, given

    def begin(at, kind):
        kept, given = copies(at, kind, core)
        kept.start()
        given.start()

    def finish(at, kind):
        kept, given = copies(at, kind, core)
        kept.wait()
        given.wait_send()

    def turned(at, who):
        tn, tk = pair(at, who)
        return tn != tk

    @pl.when(step >= 3)
    def _():
        @pl.when(turned(step - 3, core))
        def _():
            finish(step - 3, 1)

    def load(g):
        left[g] = held[:, a, g].reshape(deep, BLOCK).T

    def gram_of(g):
        block = held[:, b, g]
        crossed = jnp.concatenate([block[:, rec:], -block[:, :rec]], axis=1)
        right = jnp.concatenate(
            [block.reshape(deep, BLOCK), crossed.reshape(deep, BLOCK)], axis=1
        )
        both = jnp.dot(left[g], right, preferred_element_type=jnp.float32).astype(jnp.bfloat16)
        gram[0, g] = both[:, :BLOCK]
        gram[1, g] = both[:, BLOCK:]

    def turn(f):
        mirror[old, f, 0] = tile[old, f, 0].T
        mirror[old, f, 1] = -tile[old, f, 1].T

    per = bins // (2 * here)

    fresh = (step == 0) | (n != pair(before, core)[0])

    @pl.when((step < count) & fresh)
    def _():
        for k in range(2 * per):
            load(k)

        @pl.loop(0, here)
        def _(f):
            for k in range(2 * per):
                gram_of(f * 2 * per + k)
            turn(2 * f)
            turn(2 * f + 1)
            for k in range(2 * per):
                load(lax.rem(f + 1, here) * 2 * per + k)

    @pl.when((step < count) & jnp.logical_not(fresh))
    def _():
        @pl.loop(0, here)
        def _(f):
            for k in range(2 * per):
                gram_of(f * 2 * per + k)
            turn(2 * f)
            turn(2 * f + 1)

    @pl.when(step == count)
    def _():
        @pl.loop(0, 2 * here)
        def _(f):
            turn(f)

    @pl.when(step >= 1)
    def _():
        @pl.when(turned(before, core))
        def _():
            begin(before, 1)

    @pl.when(step >= 2)
    def _():
        finish(step - 2, 0)

    @pl.when(step < count)
    def _():
        kernel = kmat_ref[0, shift[a * blocks + b]]

        @pl.loop(0, BLOCK // SUB // 8)
        def _(part_of):
            for k in range(8):
                rows = pl.ds(pl.multiple_of((part_of * 8 + k) * SUB, SUB), SUB)
                for c in range(2):
                    part = gram[c, :, rows, :].reshape(bins * SUB, BLOCK)
                    mixed = jnp.dot(kernel, part, preferred_element_type=jnp.float32)
                    tile[slot, :, c, rows, :] = mixed.astype(jnp.bfloat16).reshape(
                        2 * here, SUB, BLOCK
                    )

        begin(step, 0)

    @pl.when(step == count)
    def _():
        finish(count - 1, 0)
        for at in (count - 2, count - 1):
            @pl.when(turned(at, core))
            def _():
                finish(at, 1)

        @pl.loop(0, count)
        def _(at):
            copies(at, 0, 1 - core)[1].wait_recv()

            @pl.when(turned(at, 1 - core))
            def _():
                copies(at, 1, 1 - core)[1].wait_recv()

        for one in own_sends():
            one.wait_send()

        @pl.when(middle)
        def _():
            for one in relays():
                one.wait_send()

        for k in range(bands):
            for one in spread(k) + pass_chip(k) + pass_side(k) + pass_corner(k):
                one.wait_send()


def fused_tiles(own, shift, kmats, groups, bands, cols, stations):
    bins, both, _ = own.shape
    here = bins // groups
    blocks = bands * cols
    count = blocks * (blocks + 1) // 4
    flops = count * bins * 2 * BLOCK * BLOCK * (groups * both * 2 + 4 * here * SUB)
    return pl.pallas_call(
        functools.partial(fused_kernel, groups, bands, cols, bins, both // 2, here),
        out_shape=jax.ShapeDtypeStruct((here, 2, stations, stations), jnp.bfloat16),
        grid_spec=pltpu.PrefetchScalarGridSpec(
            num_scalar_prefetch=1,
            grid=(count + 1,),
            in_specs=[
                pl.BlockSpec(memory_space=pl.ANY),
                pl.BlockSpec(
                    (1,) + kmats.shape[1:], lambda s, sh: (lax.axis_index("tm") // 2, 0, 0, 0)
                ),
            ],
            out_specs=pl.BlockSpec(memory_space=pl.ANY),
            scratch_shapes=[
                pltpu.VMEM((groups, blocks) + own.shape, jnp.bfloat16),
                pltpu.VMEM((bins, BLOCK, groups * both), jnp.bfloat16),
                pltpu.VMEM((2, bins, BLOCK, BLOCK), jnp.bfloat16),
                pltpu.VMEM((2, 2 * here, 2, BLOCK, BLOCK), jnp.bfloat16),
                pltpu.VMEM((2, 2 * here, 2, BLOCK, BLOCK), jnp.bfloat16),
                pltpu.SemaphoreType.DMA,
                pltpu.SemaphoreType.DMA((5 + 8 * bands,)),
                pltpu.SemaphoreType.DMA((2, groups, blocks)),
                pltpu.SemaphoreType.DMA((2, 2)),
                pltpu.SemaphoreType.DMA((2, 2)),
                pltpu.SemaphoreType.DMA((2, count)),
            ],
        ),
        compiler_params=pltpu.CompilerParams(
            vmem_limit_bytes=62 * 2**20, collective_id=1, has_side_effects=True
        ),
        cost_estimate=pl.CostEstimate(flops=flops, bytes_accessed=100 * 2**20, transcendentals=0),
        name="fused_tiles",
    )(shift, own, kmats)


def square_kernel(scale, place, rows_ref, cols_ref, out_ref):
    left_re = rows_ref[0, 0]
    left_im = rows_ref[0, 1]
    right_re = cols_ref[0, 0]
    right_im = cols_ref[0, 1]
    dot = functools.partial(jnp.dot, preferred_element_type=jnp.float32)
    squares = dot(left_re, right_re)
    crosses = dot(left_im, right_im)
    both = dot(left_re + left_im, right_re + right_im)
    out_ref[0, 0] = ((squares - crosses) * scale).astype(jnp.bfloat16)
    out_ref[1, 0] = ((both - squares - crosses) * scale).astype(jnp.bfloat16)


def square_tiles(windowed, place, tile_rows, tile_cols, scale):
    here, _, stations, _ = windowed.shape
    wide = min(512, tile_cols)
    count = tile_cols // wide
    return pl.pallas_call(
        functools.partial(square_kernel, scale),
        out_shape=jax.ShapeDtypeStruct((2, here, tile_rows, tile_cols), jnp.bfloat16),
        grid_spec=pltpu.PrefetchScalarGridSpec(
            num_scalar_prefetch=1,
            grid=(here, count),
            in_specs=[
                pl.BlockSpec((1, 2, tile_rows, stations), lambda f, j, p: (f, 0, p[0], 0)),
                pl.BlockSpec((1, 2, stations, wide), lambda f, j, p: (f, 0, 0, p[1] * count + j)),
            ],
            out_specs=pl.BlockSpec((2, 1, tile_rows, wide), lambda f, j, p: (0, f, 0, j)),
        ),
        compiler_params=pltpu.CompilerParams(vmem_limit_bytes=56 * 2**20),
        cost_estimate=pl.CostEstimate(
            flops=8 * here * tile_rows * tile_cols * stations,
            bytes_accessed=60 * 2**20,
            transcendentals=0,
        ),
        name="square_tiles",
    )(place, windowed, windowed)


def on_device(mesh, records, offsets):
    rec, _, bins, width = records.shape
    groups = mesh.shape["tm"]
    bands = mesh.shape["row"]
    stations = width * bands * mesh.shape["col"]
    here = bins // groups
    own = jnp.transpose(records, (2, 1, 0, 3)).reshape(bins, 2 * rec, width)
    cols = mesh.shape["col"]
    table = np.einsum("ofg,st->ofsgt", lag_table(bins), np.eye(SUB))
    table = table.reshape(NOFF, groups // 2, 2 * here * SUB, bins * SUB)
    kmats = jnp.asarray(np.moveaxis(table, 1, 0).astype(jnp.bfloat16))
    shift = ((offsets + offsets.T) % NOFF).reshape(-1)
    if width == BLOCK and (groups, bands, cols) == (4, 4, 2):
        windowed = fused_tiles(own, shift, kmats, groups, bands, cols, stations)
    else:
        band = lax.all_gather(own, "col", axis=2, tiled=True)
        spectra = lax.all_gather(band, ("tm", "row"), axis=0)
        spectra = spectra.reshape(groups, bands, bins, 2 * rec, stations // bands)
        kmat = lax.dynamic_index_in_dim(kmats, lax.axis_index("tm") // 2, 0, keepdims=False)
        windowed = windowed_tiles(spectra, shift, kmat, stations)
    place = jnp.stack([lax.axis_index("row"), lax.axis_index("col")]).astype(jnp.int32)
    scale = 1.0 / (rec * groups * math.sqrt(stations))
    return square_tiles(
        windowed, place, stations // bands, stations // mesh.shape["col"], scale
    )


def solution(mesh):
    return jax.shard_map(
        functools.partial(on_device, mesh),
        mesh=mesh,
        in_specs=(P("tm", None, None, ("row", "col")), P()),
        out_specs=P(None, "tm", "row", "col"),
        check_vma=False,
    )
```

```python
import functools
import math

import jax
import jax.numpy as jnp
import numpy as np
from jax import lax
from jax.experimental import pallas as pl
from jax.experimental.pallas import tpu as pltpu
from jax.sharding import PartitionSpec as P

BLOCK = 256
NOFF = 4
SUB = 16


def lag_table(bins):
    freq = np.arange(bins)
    lag = np.minimum(freq, bins - freq)
    starts = np.arange(NOFF)[:, None] + 2
    inside = (lag[None, :] >= starts) & (lag[None, :] < starts + 3)
    weights = np.where(inside, 1.0, 0.1)
    phase = (freq[:, None, None] - freq[None, :, None]) * freq[None, None, :] % bins
    cosines = np.cos(phase * (2.0 * math.pi / bins))
    return np.einsum("ot,fgt->ofg", weights, cosines) / bins


def pair_of(step, core, blocks):
    half = blocks // 2
    main = half * half
    tail = step // main
    row = (step // half) * (1 - tail) + (step - main) * tail
    return core * (half - half // 2 * tail) + row, (step % half) * (1 - tail) + half * tail


def tile_kernel(bins, groups, rec, here, blocks, shift, xa_ref, xb_ref, kmat_ref,
                out_ref, left, gram, tile, mirror, local_sem, send_sem, recv_sem):
    step = pl.program_id(0)
    count = pl.num_programs(0) - 1
    tm = lax.axis_index("tm")
    core = lax.rem(tm, 2)
    partner = tm + 1 - 2 * core
    half = blocks // 2
    deep = groups * 2 * rec
    slot = lax.rem(step, 2)
    a, d = pair_of(jnp.minimum(step, count - 1), core, blocks)
    b = lax.rem(a + d, blocks)

    def copies(at, kind):
        ta, td = pair_of(at, core, blocks)
        tb = lax.rem(ta + td, blocks)
        where = lax.rem(at, 2)
        first, second = (ta, tb) if kind == 0 else (tb, ta)
        rows = pl.ds(pl.multiple_of(first * BLOCK, BLOCK), BLOCK)
        cols = pl.ds(pl.multiple_of(second * BLOCK, BLOCK), BLOCK)
        held = tile if kind == 0 else mirror
        kept = pltpu.make_async_copy(
            held.at[where, pl.ds(core * here, here)], out_ref.at[:, :, rows, cols],
            local_sem.at[kind, where],
        )
        given = pltpu.make_async_remote_copy(
            src_ref=held.at[where, pl.ds((1 - core) * here, here)],
            dst_ref=out_ref.at[:, :, rows, cols],
            send_sem=send_sem.at[kind, where],
            recv_sem=recv_sem.at[kind, at],
            device_id={"tm": partner},
            device_id_type=pl.DeviceIdType.MESH,
        )
        return kept, given

    def begin(at, kind):
        kept, given = copies(at, kind)
        kept.start()
        given.start()

    def finish(at, kind):
        kept, given = copies(at, kind)
        kept.wait()
        given.wait_send()

    def turned(at):
        return pair_of(at, core, blocks)[1] > 0

    @pl.when(step == 0)
    def _():
        barrier = pltpu.get_barrier_semaphore()
        pl.semaphore_signal(
            barrier, inc=1, device_id={"tm": partner}, device_id_type=pl.DeviceIdType.MESH
        )
        pl.semaphore_wait(barrier, 1)

    @pl.when((step < count) & ((d == 0) | (step >= half * half)))
    def _():
        @pl.loop(0, bins)
        def _(g):
            block = xa_ref[:, 0, g]
            crossed = jnp.concatenate([-block[:, rec:], block[:, :rec]], axis=1)
            left[g, :BLOCK] = block.reshape(deep, BLOCK).T
            left[g, BLOCK:] = crossed.reshape(deep, BLOCK).T

    before = jnp.maximum(step - 1, 0)
    old = lax.rem(step + 1, 2)

    @pl.when(step >= 3)
    def _():
        @pl.when(turned(step - 3))
        def _():
            finish(step - 3, 1)

    def gram_of(g):
        both = jnp.dot(
            left[g], xb_ref[:, 0, g].reshape(deep, BLOCK), preferred_element_type=jnp.float32
        ).astype(jnp.bfloat16)
        gram[0, g] = both[:BLOCK]
        gram[1, g] = both[BLOCK:]

    def turn(f):
        mirror[old, f, 0] = tile[old, f, 0].T
        mirror[old, f, 1] = -tile[old, f, 1].T

    per = bins // (2 * here)

    @pl.when(step < count)
    def _():
        @pl.loop(0, 2 * here)
        def _(f):
            for k in range(per):
                gram_of(f * per + k)
            turn(f)

    @pl.when(step == count)
    def _():
        @pl.loop(0, 2 * here)
        def _(f):
            turn(f)

    @pl.when(step >= 1)
    def _():
        @pl.when(turned(before))
        def _():
            begin(before, 1)

    @pl.when(step >= 2)
    def _():
        finish(step - 2, 0)

    @pl.when(step < count)
    def _():
        kernel = kmat_ref[shift[a * blocks + b]]

        @pl.loop(0, BLOCK // SUB // 4)
        def _(quad):
            for k in range(4):
                rows = pl.ds(pl.multiple_of((quad * 4 + k) * SUB, SUB), SUB)
                for c in range(2):
                    part = gram[c, :, rows, :].reshape(bins * SUB, BLOCK)
                    mixed = jnp.dot(kernel, part, preferred_element_type=jnp.float32)
                    tile[slot, :, c, rows, :] = mixed.astype(jnp.bfloat16).reshape(
                        2 * here, SUB, BLOCK
                    )

        begin(step, 0)

    @pl.when(step == count)
    def _():
        finish(count - 1, 0)
        for at in (count - 2, count - 1):
            @pl.when(turned(at))
            def _():
                finish(at, 1)

        @pl.loop(0, count)
        def _(at):
            copies(at, 0)[1].wait_recv()

            @pl.when(turned(at))
            def _():
                copies(at, 1)[1].wait_recv()


def windowed_tiles(spectra, shift, kmat, stations):
    groups, bands, bins, both, width = spectra.shape
    rec = both // 2
    here = bins // groups
    per = width // BLOCK
    blocks = stations // BLOCK
    count = blocks * (blocks + 1) // 4
    block = (groups, 1, bins, both, BLOCK)
    flops = count * bins * 2 * BLOCK * BLOCK * (groups * both * 2 + 4 * here * SUB)

    def pick_a(s, sh):
        a, _ = pair_of(jnp.minimum(s, count - 1), lax.rem(lax.axis_index("tm"), 2), blocks)
        return (0, a // per, 0, 0, lax.rem(a, per))

    def pick_b(s, sh):
        a, d = pair_of(jnp.minimum(s, count - 1), lax.rem(lax.axis_index("tm"), 2), blocks)
        b = lax.rem(a + d, blocks)
        return (0, b // per, 0, 0, lax.rem(b, per))

    return pl.pallas_call(
        functools.partial(tile_kernel, bins, groups, rec, here, blocks),
        out_shape=jax.ShapeDtypeStruct((here, 2, stations, stations), jnp.bfloat16),
        grid_spec=pltpu.PrefetchScalarGridSpec(
            num_scalar_prefetch=1,
            grid=(count + 1,),
            in_specs=[
                pl.BlockSpec(block, pick_a),
                pl.BlockSpec(block, pick_b),
                pl.BlockSpec(kmat.shape, lambda s, sh: (0, 0, 0)),
            ],
            out_specs=pl.BlockSpec(memory_space=pl.ANY),
            scratch_shapes=[
                pltpu.VMEM((bins, 2 * BLOCK, groups * both), jnp.bfloat16),
                pltpu.VMEM((2, bins, BLOCK, BLOCK), jnp.bfloat16),
                pltpu.VMEM((2, 2 * here, 2, BLOCK, BLOCK), jnp.bfloat16),
                pltpu.VMEM((2, 2 * here, 2, BLOCK, BLOCK), jnp.bfloat16),
                pltpu.SemaphoreType.DMA((2, 2)),
                pltpu.SemaphoreType.DMA((2, 2)),
                pltpu.SemaphoreType.DMA((2, count)),
            ],
        ),
        compiler_params=pltpu.CompilerParams(
            vmem_limit_bytes=60 * 2**20, collective_id=0, has_side_effects=True
        ),
        cost_estimate=pl.CostEstimate(flops=flops, bytes_accessed=200 * 2**20, transcendentals=0),
        name="windowed_tiles",
    )(shift, spectra, spectra, kmat)


def fused_kernel(groups, bands, cols, bins, rec, here, shift, own_ref, kmat_ref, out_ref,
                 held, left, gram, tile, mirror, own_sem, piece_send, piece_recv,
                 local_sem, send_sem, recv_sem):
    step = pl.program_id(0)
    count = pl.num_programs(0) - 1
    tm = lax.axis_index("tm")
    row = lax.axis_index("row")
    col = lax.axis_index("col")
    core = lax.rem(tm, 2)
    partner = tm + 1 - 2 * core
    blocks = bands * cols
    deep = groups * 2 * rec
    slot = lax.rem(step, 2)
    old = lax.rem(step + 1, 2)
    mesh_id = pl.DeviceIdType.MESH
    chip = lax.rem(tm + 2, groups)
    side = lax.rem(col + 1, cols)
    bin_half = bins // 2
    middle = (row == 1) | (row == 2)
    arrival = [(0, 0), (1, 0), (0, 1), (2, 0), (1, 1), (3, 0), (2, 1), (3, 1)]

    def row_at(k):
        high = row // 2
        return (row, row + 1 - 2 * lax.rem(row, 2), 2 - high, 3 - 3 * high)[k]

    def block_at(n):
        total = 0
        for index, (k, other) in enumerate(arrival):
            where = row_at(k) * cols + (side if other else col)
            total = total + jnp.where(n == index, where, 0)
        return total

    def pair(at, who):
        t = 2 * at + who
        n = 0
        for index in range(1, blocks):
            n = n + jnp.minimum(t // (index * (index + 1) // 2), 1)
        return n, t - n * (n + 1) // 2

    def send(index, t, k, q, target, part=None, source=None):
        block = row_at(k) * cols + q
        there = held.at[t, block]
        source = there if source is None else source
        if part is not None:
            source = source.at[pl.ds(part * bin_half, bin_half)]
            there = there.at[pl.ds(part * bin_half, bin_half)]
        return pltpu.make_async_remote_copy(
            src_ref=source, dst_ref=there, send_sem=piece_send.at[index],
            recv_sem=piece_recv.at[part or 0, t, block], device_id=target, device_id_type=mesh_id,
        )

    def arrive(t, k, q, part=None):
        block = row_at(k) * cols + q
        piece = held.at[t, block]
        if part is not None:
            piece = piece.at[pl.ds(part * bin_half, bin_half)]
        pltpu.make_async_copy(piece, piece, piece_recv.at[part or 0, t, block]).wait()

    def own_sends():
        return [send(0, tm, 0, col, {"row": row_at(1)}, source=own_ref)]

    def relays():
        over, back = {"row": row_at(2)}, {"row": row_at(1)}
        return [
            send(1, tm, 0, col, over, source=own_ref),
            send(2, tm, 1, col, over),
            send(3, tm, 2, col, back),
            send(4, tm, 3, col, back),
        ]

    def spread(k):
        source = own_ref if k == 0 else None
        base = 5 + 8 * k
        return [
            send(base, tm, k, col, {"tm": chip}, source=source),
            send(base + 1, tm, k, col, {"col": side}, source=source),
            send(base + 2, tm, k, col, {"tm": partner}, source=source),
        ]

    def pass_chip(k):
        base = 8 + 8 * k
        return [
            send(base, chip, k, col, {"col": side}, 0),
            send(base + 1, chip, k, col, {"tm": partner}),
        ]

    def pass_side(k):
        base = 10 + 8 * k
        return [
            send(base, tm, k, side, {"tm": chip}, 1),
            send(base + 1, tm, k, side, {"tm": partner}),
        ]

    def pass_corner(k):
        return [send(12 + 8 * k, chip, k, side, {"tm": partner})]

    def start(copies):
        for one in copies:
            one.start()

    def relay(k):
        @pl.when(middle)
        def _():
            relays()[k].start()

    def row_piece(k):
        arrive(tm, k, col)
        relay(k)
        start(spread(k))

    def edge_pieces(k):
        arrive(chip, k, col)
        start(pass_chip(k))
        arrive(tm, k, side)
        start(pass_side(k))

    def corner_piece(k):
        arrive(chip, k, side, 0)
        arrive(chip, k, side, 1)
        start(pass_corner(k))

    def from_core(k, q):
        arrive(partner, k, q)
        arrive(lax.rem(partner + 2, groups), k, q)

    mine = pltpu.make_async_copy(own_ref, held.at[tm, row * cols + col], own_sem)

    @pl.when(step == 0)
    def _():
        barrier = pltpu.get_barrier_semaphore()
        friends = [{"tm": chip}, {"col": side}, {"tm": partner}]
        friends += [{"row": row_at(k)} for k in (1, 2, 3)]
        for friend in friends:
            pl.semaphore_signal(barrier, inc=1, device_id=friend, device_id_type=mesh_id)
        pl.semaphore_wait(barrier, len(friends))
        start(own_sends())
        relay(0)
        start(spread(0))
        mine.start()
        row_piece(1)
        edge_pieces(0)
        row_piece(2)
        mine.wait()
        edge_pieces(1)
        from_core(0, col)
        from_core(1, col)

    @pl.when(step == 1)
    def _():
        corner_piece(0)
        row_piece(3)
        from_core(0, side)

    @pl.when(step == 3)
    def _():
        edge_pieces(2)
        from_core(2, col)

    @pl.when(step == 5)
    def _():
        corner_piece(1)
        from_core(1, side)

    @pl.when(step == 7)
    def _():
        edge_pieces(3)
        from_core(3, col)

    @pl.when(step == 10)
    def _():
        corner_piece(2)
        from_core(2, side)

    @pl.when(step == 14)
    def _():
        corner_piece(3)
        from_core(3, side)

    now = jnp.minimum(step, count - 1)
    n, m = pair(now, core)
    a = block_at(n)
    b = block_at(m)
    before = jnp.maximum(step - 1, 0)

    def copies(at, kind, who):
        tn, tk = pair(at, who)
        first, second = (tn, tk) if kind == 0 else (tk, tn)
        where = lax.rem(at, 2)
        rows = pl.ds(pl.multiple_of(block_at(first) * BLOCK, BLOCK), BLOCK)
        columns = pl.ds(pl.multiple_of(block_at(second) * BLOCK, BLOCK), BLOCK)
        source = tile if kind == 0 else mirror
        kept = pltpu.make_async_copy(
            source.at[where, pl.ds(core * here, here)], out_ref.at[:, :, rows, columns],
            local_sem.at[kind, where],
        )
        given = pltpu.make_async_remote_copy(
            src_ref=source.at[where, pl.ds((1 - core) * here, here)],
            dst_ref=out_ref.at[:, :, rows, columns],
            send_sem=send_sem.at[kind, where],
            recv_sem=recv_sem.at[kind, at],
            device_id={"tm": partner},
            device_id_type=mesh_id,
        )
        return kept, given

    def begin(at, kind):
        kept, given = copies(at, kind, core)
        kept.start()
        given.start()

    def finish(at, kind):
        kept, given = copies(at, kind, core)
        kept.wait()
        given.wait_send()

    def turned(at, who):
        tn, tk = pair(at, who)
        return tn != tk

    @pl.when(step >= 3)
    def _():
        @pl.when(turned(step - 3, core))
        def _():
            finish(step - 3, 1)

    def load(g):
        left[g] = held[:, a, g].reshape(deep, BLOCK).T

    def gram_of(g):
        block = held[:, b, g]
        crossed = jnp.concatenate([block[:, rec:], -block[:, :rec]], axis=1)
        right = jnp.concatenate(
            [block.reshape(deep, BLOCK), crossed.reshape(deep, BLOCK)], axis=1
        )
        both = jnp.dot(left[g], right, preferred_element_type=jnp.float32).astype(jnp.bfloat16)
        gram[0, g] = both[:, :BLOCK]
        gram[1, g] = both[:, BLOCK:]

    def turn(f):
        mirror[old, f, 0] = tile[old, f, 0].T
        mirror[old, f, 1] = -tile[old, f, 1].T

    fresh = (step == 0) | (n != pair(before, core)[0])

    @pl.when((step < count) & fresh)
    def _():
        for k in range(bins // 2):
            load(k)

        @pl.loop(0, 2)
        def _(part_of):
            for k in range(bins // 2):
                gram_of(part_of * (bins // 2) + k)
            for k in range(here):
                turn(part_of * here + k)
            for k in range(bins // 2):
                load((1 - part_of) * (bins // 2) + k)

    @pl.when((step < count) & jnp.logical_not(fresh))
    def _():
        @pl.loop(0, 2)
        def _(part_of):
            for k in range(bins // 2):
                gram_of(part_of * (bins // 2) + k)
            for k in range(here):
                turn(part_of * here + k)

    @pl.when(step == count)
    def _():
        @pl.loop(0, 2 * here)
        def _(f):
            turn(f)

    @pl.when(step >= 1)
    def _():
        @pl.when(turned(before, core))
        def _():
            begin(before, 1)

    @pl.when(step >= 2)
    def _():
        finish(step - 2, 0)

    @pl.when(step < count)
    def _():
        kernel = kmat_ref[0, shift[a * blocks + b]]

        for k in range(BLOCK // SUB):
            rows = pl.ds(k * SUB, SUB)
            for c in range(2):
                part = gram[c, :, rows, :].reshape(bins * SUB, BLOCK)
                mixed = jnp.dot(kernel, part, preferred_element_type=jnp.float32)
                tile[slot, :, c, rows, :] = mixed.astype(jnp.bfloat16).reshape(
                    2 * here, SUB, BLOCK
                )

        begin(step, 0)

    @pl.when(step == count)
    def _():
        finish(count - 1, 0)
        for at in (count - 2, count - 1):
            @pl.when(turned(at, core))
            def _():
                finish(at, 1)

        @pl.loop(0, count)
        def _(at):
            copies(at, 0, 1 - core)[1].wait_recv()

            @pl.when(turned(at, 1 - core))
            def _():
                copies(at, 1, 1 - core)[1].wait_recv()

        for one in own_sends():
            one.wait_send()

        @pl.when(middle)
        def _():
            for one in relays():
                one.wait_send()

        for k in range(bands):
            for one in spread(k) + pass_chip(k) + pass_side(k) + pass_corner(k):
                one.wait_send()


def fused_tiles(own, shift, kmats, groups, bands, cols, stations):
    bins, both, _ = own.shape
    here = bins // groups
    blocks = bands * cols
    count = blocks * (blocks + 1) // 4
    flops = count * bins * 2 * BLOCK * BLOCK * (groups * both * 2 + 4 * here * SUB)
    return pl.pallas_call(
        functools.partial(fused_kernel, groups, bands, cols, bins, both // 2, here),
        out_shape=jax.ShapeDtypeStruct((here, 2, stations, stations), jnp.bfloat16),
        grid_spec=pltpu.PrefetchScalarGridSpec(
            num_scalar_prefetch=1,
            grid=(count + 1,),
            in_specs=[
                pl.BlockSpec(memory_space=pl.ANY),
                pl.BlockSpec(
                    (1,) + kmats.shape[1:], lambda s, sh: (lax.axis_index("tm") // 2, 0, 0, 0)
                ),
            ],
            out_specs=pl.BlockSpec(memory_space=pl.ANY),
            scratch_shapes=[
                pltpu.VMEM((groups, blocks) + own.shape, jnp.bfloat16),
                pltpu.VMEM((bins, BLOCK, groups * both), jnp.bfloat16),
                pltpu.VMEM((2, bins, BLOCK, BLOCK), jnp.bfloat16),
                pltpu.VMEM((2, 2 * here, 2, BLOCK, BLOCK), jnp.bfloat16),
                pltpu.VMEM((2, 2 * here, 2, BLOCK, BLOCK), jnp.bfloat16),
                pltpu.SemaphoreType.DMA,
                pltpu.SemaphoreType.DMA((5 + 8 * bands,)),
                pltpu.SemaphoreType.DMA((2, groups, blocks)),
                pltpu.SemaphoreType.DMA((2, 2)),
                pltpu.SemaphoreType.DMA((2, 2)),
                pltpu.SemaphoreType.DMA((2, count)),
            ],
        ),
        compiler_params=pltpu.CompilerParams(
            vmem_limit_bytes=62 * 2**20, collective_id=1, has_side_effects=True
        ),
        cost_estimate=pl.CostEstimate(flops=flops, bytes_accessed=100 * 2**20, transcendentals=0),
        name="fused_tiles",
    )(shift, own, kmats)


def square_kernel(scale, place, rows_ref, cols_ref, out_ref):
    left_re = rows_ref[0, 0]
    left_im = rows_ref[0, 1]
    right_re = cols_ref[0, 0]
    right_im = cols_ref[0, 1]
    dot = functools.partial(jnp.dot, preferred_element_type=jnp.float32)
    squares = dot(left_re, right_re)
    crosses = dot(left_im, right_im)
    both = dot(left_re + left_im, right_re + right_im)
    out_ref[0, 0] = ((squares - crosses) * scale).astype(jnp.bfloat16)
    out_ref[1, 0] = ((both - squares - crosses) * scale).astype(jnp.bfloat16)


def square_tiles(windowed, place, tile_rows, tile_cols, scale):
    here, _, stations, _ = windowed.shape
    wide = min(512, tile_cols)
    count = tile_cols // wide
    return pl.pallas_call(
        functools.partial(square_kernel, scale),
        out_shape=jax.ShapeDtypeStruct((2, here, tile_rows, tile_cols), jnp.bfloat16),
        grid_spec=pltpu.PrefetchScalarGridSpec(
            num_scalar_prefetch=1,
            grid=(here, count),
            in_specs=[
                pl.BlockSpec((1, 2, tile_rows, stations), lambda f, j, p: (f, 0, p[0], 0)),
                pl.BlockSpec((1, 2, stations, wide), lambda f, j, p: (f, 0, 0, p[1] * count + j)),
            ],
            out_specs=pl.BlockSpec((2, 1, tile_rows, wide), lambda f, j, p: (0, f, 0, j)),
        ),
        compiler_params=pltpu.CompilerParams(vmem_limit_bytes=56 * 2**20),
        cost_estimate=pl.CostEstimate(
            flops=8 * here * tile_rows * tile_cols * stations,
            bytes_accessed=60 * 2**20,
            transcendentals=0,
        ),
        name="square_tiles",
    )(place, windowed, windowed)


def on_device(mesh, records, offsets):
    rec, _, bins, width = records.shape
    groups = mesh.shape["tm"]
    bands = mesh.shape["row"]
    stations = width * bands * mesh.shape["col"]
    here = bins // groups
    own = jnp.transpose(records, (2, 1, 0, 3)).reshape(bins, 2 * rec, width)
    cols = mesh.shape["col"]
    table = np.einsum("ofg,st->ofsgt", lag_table(bins), np.eye(SUB))
    table = table.reshape(NOFF, groups // 2, 2 * here * SUB, bins * SUB)
    kmats = jnp.asarray(np.moveaxis(table, 1, 0).astype(jnp.bfloat16))
    shift = ((offsets + offsets.T) % NOFF).reshape(-1)
    if width == BLOCK and (groups, bands, cols) == (4, 4, 2):
        windowed = fused_tiles(own, shift, kmats, groups, bands, cols, stations)
    else:
        band = lax.all_gather(own, "col", axis=2, tiled=True)
        spectra = lax.all_gather(band, ("tm", "row"), axis=0)
        spectra = spectra.reshape(groups, bands, bins, 2 * rec, stations // bands)
        kmat = lax.dynamic_index_in_dim(kmats, lax.axis_index("tm") // 2, 0, keepdims=False)
        windowed = windowed_tiles(spectra, shift, kmat, stations)
    place = jnp.stack([lax.axis_index("row"), lax.axis_index("col")]).astype(jnp.int32)
    scale = 1.0 / (rec * groups * math.sqrt(stations))
    return square_tiles(
        windowed, place, stations // bands, stations // mesh.shape["col"], scale
    )


def solution(mesh):
    return jax.shard_map(
        functools.partial(on_device, mesh),
        mesh=mesh,
        in_specs=(P("tm", None, None, ("row", "col")), P()),
        out_specs=P(None, "tm", "row", "col"),
        check_vma=False,
    )
```
